768 devices in a mesh: strip: 12 (over z), tile: 64 (over x, y, core).
Axes of the slice: x: 4, y: 8, z: 12, core: 2. Of those that a mesh axis runs over, the one named last changes fastest.
Arguments:
- coords: float32 [36864, 3, 128], P(('strip', 'tile')), may hold values from -0.25 to 12288.25, as said below
- displacement: float32 [36864, 3, 128], P(('strip', 'tile')), may hold values from -0.75 to 0.75
- pairs: int32 [49152, 2], P(('strip', 'tile')), may hold values from 0 to 36863, as said below
- intact: int32 [49152, 128, 128], P(('strip', 'tile')), may hold values 0 or 1
Outputs:
- force: float32 [36864, 3, 128], P(('strip', 'tile'))
The draws below stay inside these ranges and needn't reach their ends.
Inputs may be any that keep to these rules, and one draw needn't show every extreme that they name: `coords`: each point sits within 0.25 of its lattice site: tile t covers a 4 x 4 x 8 block of unit lattice sites starting at (4 (t // 3072), 4 (t % 3072), 0), point i at offset (i % 4, (i // 4) % 4, i // 16). `pairs`: the rows of one device (device number d = strip index * 64 + tile index) name as first tile one of the 48 tiles that this device holds, and as second tile a different one whose strip differs from the first's by at most one and whose place within its strip differs from the first's place within its strip by at most one.
All inputs are finite; a program needn't handle non-finite values. No bound on the sum of `intact` on one device may be relied on, other than what follows from the above.
Results may differ from the reference program's by a relative error of at most 0.0003.
Values sent between devices are 32-bit elements; how exact they have to be, the bound alone decides.
No kernel may reach another device: no remote copies, remote signals or barrier semaphores. Data moves between devices by JAX's collectives and lax.ppermute only.
A program may use at most 32 MiB of HBM per device.

```python
import math
import jax
import jax.numpy as jnp
from jax import lax

TILE = 128
TPD = 48
PAIRS_DEV = 64
TILES_STRIP = 3072
TILES = 36864
PAIRS = 49152
N_STRIP = 12
N_TILE = 64


def draw_coords(key, part):
    tile_ids = jnp.arange(TILES)[:, None]
    point_ids = jnp.arange(TILE)[None, :]
    across = 4 * (tile_ids // TILES_STRIP) + point_ids % 4
    along = 4 * (tile_ids % TILES_STRIP) + point_ids // 4 % 4
    depth = point_ids // 16 + 0 * tile_ids
    lattice = jnp.stack([across, along, depth], axis=1).astype(jnp.float32)
    jitter = jax.random.uniform(key, lattice.shape, jnp.float32, -0.2, 0.2)
    return lattice + jitter


def draw_pairs(key, part):
    keys = jax.random.split(jax.random.fold_in(key, 17), 3)
    rows = jnp.arange(PAIRS)
    strip_of = rows // (PAIRS_DEV * N_TILE)
    device_in_strip = rows // PAIRS_DEV % N_TILE
    first_local = device_in_strip * TPD + jax.random.randint(keys[0], (PAIRS,), 0, TPD)
    side = jax.random.randint(keys[1], (PAIRS,), -1, 2)
    offset = jax.random.randint(keys[2], (PAIRS,), -1, 2)
    second_strip = jnp.clip(strip_of + side, 0, N_STRIP - 1)
    second_local = jnp.clip(first_local + offset, 0, TILES_STRIP - 1)
    same = (second_strip == strip_of) & (second_local == first_local)
    moved_local = jnp.where(first_local + 1 < TILES_STRIP, first_local + 1, first_local - 1)
    second_local = jnp.where(same, moved_local, second_local)
    first_tile = strip_of * TILES_STRIP + first_local
    second_tile = second_strip * TILES_STRIP + second_local
    return jnp.stack([first_tile, second_tile], axis=1).astype(jnp.int32)


def touch_ends(drawn, rng, low, high):
    longest = drawn.shape.index(max(drawn.shape))
    spots = []
    for shift in (0, 1):
        where = [jax.random.randint(jax.random.fold_in(rng, axis), (), 0, length) for axis, length in enumerate(drawn.shape)]
        where[longest] = (where[longest] + shift) % drawn.shape[longest]
        spots.append(tuple(where))
    return drawn.at[spots[0]].set(low).at[spots[1]].set(high)


def block_scale(own_key, extent, shards, smallest, top_value):
    level = 1.0
    for position, parts in shards:
        draws = jax.random.uniform(jax.random.fold_in(jax.random.fold_in(own_key, 6), position), (parts,), jnp.float32, smallest / len(shards), top_value / len(shards))
        level = level * jnp.repeat(jnp.exp(draws), extent[position] // parts).reshape((-1,) + (1,) * (len(extent) - 1 - position))
    return level


def gaussian(rng, extent, deviation, limit, pieces=(), kind=jnp.bfloat16):
    result = deviation * jax.random.normal(rng, extent, jnp.float32)
    if pieces:
        result = result * block_scale(rng, extent, pieces, -0.22, 0.18)
    return jnp.clip(result, -limit, limit).astype(kind)


def setup_inputs(seed: int = 0) -> dict:
    key_list = jax.random.split(jax.random.key(seed), 5)
    return {
        "coords": draw_coords(jax.random.fold_in(key_list[4], 71), 0),
        "displacement": gaussian(key_list[1], (TILES, 3, TILE), 0.05, 0.75, ((0, 768),), jnp.float32),
        "pairs": draw_pairs(jax.random.fold_in(key_list[4], 71), 0),
        "intact": touch_ends((jax.random.randint(key_list[3], (PAIRS, TILE, TILE), 0, 8) < 7).astype(jnp.int32), jax.random.fold_in(key_list[3], 1), 0, 1),
    }


horizon = 3.0
stiffness = 2.0
onset_stretch = 0.02
final_stretch = 0.05

def block_forces(first_block, second, bond_mask):
    bond_ref = second[0:3, None, :] - first_block[0:3, :, None]
    bond_now = bond_ref + second[3:6, None, :] - first_block[3:6, :, None]
    length_ref = jnp.sqrt(lax.optimization_barrier(jnp.sum(bond_ref * bond_ref, axis=0)))
    length_now = jnp.sqrt(lax.optimization_barrier(jnp.sum(bond_now * bond_now, axis=0)))
    stretch = (length_now - length_ref) / length_ref
    influence = jnp.maximum(0.0, 1.0 - length_ref / horizon)
    soften = jnp.clip((final_stretch - stretch) / (final_stretch - onset_stretch), 0.0, 1.0)
    pull_scale = stiffness * stretch * influence * soften * bond_mask.astype(jnp.float32) / length_now
    bond_force = pull_scale[None] * bond_now
    return (lax.optimization_barrier(jnp.sum(bond_force, axis=2)), -lax.optimization_barrier(jnp.sum(bond_force, axis=1)))

def reference(coords, displacement, pairs, intact):
    point_table = jnp.concatenate([coords, displacement], axis=1)
    group_size = math.gcd(pairs.shape[0], 8)
    grouped_pairs = pairs.reshape(-1, group_size, 2)
    grouped_bonds = intact.reshape(-1, group_size, intact.shape[1], intact.shape[2])

    def visit(forces, scan_item):
        couple, bond_mask = scan_item
        first_ids = couple[:, 0].astype(jnp.int32)
        second_ids = couple[:, 1].astype(jnp.int32)
        gain_first, gain_second = jax.vmap(block_forces)(point_table[first_ids], point_table[second_ids], bond_mask)
        forces = forces.at[first_ids].add(gain_first)
        forces = forces.at[second_ids].add(gain_second)
        return (forces, None)
    zero_forces = jnp.zeros(coords.shape, coords.dtype)
    forces, unused = lax.scan(visit, zero_forces, (grouped_pairs, grouped_bonds))
    return forces
```

```python
import functools

import jax
import jax.numpy as jnp
from jax import lax
from jax.experimental import pallas as pl
from jax.experimental.pallas import tpu as pltpu
from jax.sharding import PartitionSpec as P

HORIZON = 3.0
STIFFNESS = 2.0
ONSET = 0.02
FINAL = 0.05

GROUP = 4
VMEM = pl.BlockSpec(memory_space=pltpu.VMEM)
HBM = pl.BlockSpec(memory_space=pltpu.HBM)
SMEM = pl.BlockSpec(memory_space=pltpu.SMEM)


def shifted(value, axis, step):
    count = lax.axis_size(axis)
    first, last = max(0, -step), min(count, count - step)
    return lax.ppermute(value, axis, [(i, i + step) for i in range(first, last)])


def in_hbm(value):
    return pltpu.with_memory_space_constraint(value, pltpu.HBM)


def padded_rows(rows):
    return (rows + 7) // 8 * 8


def pack_kernel(held, coords, displacement, out, first, last, arrived):
    rows = 3 * held
    copies = [
        pltpu.make_async_copy(source, out.at[pl.ds(i * rows, rows)], arrived.at[i])
        for i, source in enumerate((coords, displacement))
    ]
    for copy in copies:
        copy.start()
    out[2 * rows :] = jnp.zeros((out.shape[0] - 2 * rows, out.shape[1]), jnp.float32)
    for copy in copies:
        copy.wait()
    for t, edge in ((0, first), (held - 1, last)):
        edge[...] = out[pl.ds(t, 6, stride=held)]


def frame_kernel(held, payload, left, right, out):
    out[6 * held : 6 * held + 6] = left[...]
    out[6 * held + 6 : 6 * held + 12] = right[...]


def pieces(value):
    first = value.astype(jnp.bfloat16).astype(jnp.float32)
    rest = value - first
    second = rest.astype(jnp.bfloat16).astype(jnp.float32)
    return first, second, rest - second


def side_rows(tile, middle, row):
    here = tile - middle
    moved = pltpu.roll(here, 5, axis=0)
    now = here + moved
    low = row < 3
    square = jnp.sum(jnp.where(low, here * here, 0.0), axis=0, keepdims=True)
    growth = jnp.sum(jnp.where(low, moved * (here + now), 0.0), axis=0, keepdims=True)
    return here, moved, now, square, growth


def now_rows(now, row):
    first = now.astype(jnp.bfloat16).astype(jnp.float32)
    second = now - first
    top = jnp.where(row < 3, first, jnp.where(row == 3, 1.0, 0.0))
    rows = jnp.concatenate([top, jnp.where(row < 3, second, 0.0)], axis=0)
    rows = rows.astype(jnp.bfloat16)
    return jnp.concatenate([rows, rows], axis=1)


def pair_forces(tile_a, tile_b, mid_x, mid_y, bond_mask, mid_z):
    points = tile_a.shape[-1]
    row = lax.broadcasted_iota(jnp.int32, (8, points), 0)
    middle = jnp.where(
        row == 0, mid_x, jnp.where(row == 1, mid_y, jnp.where(row == 2, mid_z, 0.0))
    )
    here_a, _, now_a, square_a, growth_a = side_rows(tile_a, middle, row)
    here_b, moved_b, now_b, square_b, growth_b = side_rows(tile_b, middle, row)

    six, seven = row == 6, row == 7
    left = jnp.where(row < 6, -2.0 * here_a, jnp.where(six, square_a, growth_a))
    l1, l2, l3 = pieces(left)

    def ones(value):
        return jnp.where(row < 6, value, jnp.where(six, 1.0, 0.0))

    o1, o2 = ones(l1), ones(l2)
    lhs = jnp.concatenate([l1, l2, l3, o1, o2, o1], axis=0).astype(jnp.bfloat16)

    shifted_b = pltpu.roll(now_b, 3, axis=0)
    right_ref = jnp.where(row < 3, here_b, jnp.where(six, square_b, 0.0))
    right_gain = jnp.where(
        row < 3, moved_b, jnp.where(row < 6, shifted_b, jnp.where(six, growth_b, 0.0))
    )

    def stack(value, at_six, at_seven):
        p1, p2, p3 = pieces(value)
        base = jnp.where(six, at_six, jnp.where(seven, at_seven, p1))
        mixed = jnp.where(six, p1, p2)
        return jnp.concatenate([base, base, base, mixed, p2, p3], axis=0)

    rhs = jnp.concatenate([stack(right_ref, 1.0, 0.0), stack(right_gain, 0.0, 1.0)], axis=1)
    both = lax.dot_general(
        lhs, rhs.astype(jnp.bfloat16), (((0,), (0,)), ((), ())), preferred_element_type=jnp.float32
    )
    ref2, gain2 = both[:, :points], both[:, points:]

    now2 = jnp.maximum(ref2 + gain2, 1e-6)
    per_ref, per_now = lax.rsqrt(ref2), lax.rsqrt(now2)
    length_ref, length_now = ref2 * per_ref, now2 * per_now
    stretch = gain2 * per_ref / (length_now + length_ref)
    influence = jnp.maximum(1.0 - length_ref * (1.0 / HORIZON), 0.0)
    spread = FINAL - ONSET
    soften = jnp.clip(FINAL / spread - stretch * (1.0 / spread), 0.0, 1.0)
    pull = (
        (STIFFNESS * stretch) * (influence * soften) * (per_now * bond_mask.astype(jnp.float32))
    )
    high = pull.astype(jnp.bfloat16)
    low = (pull - high.astype(jnp.float32)).astype(jnp.bfloat16)

    on_b = jnp.dot(
        now_rows(now_a, row),
        jnp.concatenate([high, low], axis=0),
        preferred_element_type=jnp.float32,
    )
    on_a = lax.dot_general(
        now_rows(now_b, row),
        jnp.concatenate([high, low], axis=1),
        (((1,), (1,)), ((), ())),
        preferred_element_type=jnp.float32,
    )
    sum_a, sum_b = on_a[0:8] + on_a[8:16], on_b[0:8] + on_b[8:16]
    return sum_a - now_a * sum_a[3:4], sum_b - now_b * sum_b[3:4]


def bond_kernel(mid_z, held, info, below, own, above, intact, force, down, up, edges, table, total, held_bonds, arrived):
    count = intact.shape[0]
    steps = count // GROUP

    def bonds(step):
        part = pl.ds(step * GROUP, GROUP)
        return pltpu.make_async_copy(intact.at[part], held_bonds.at[part], arrived.at[step])

    for step in range(steps):
        bonds(step).start()
    span = held + 2
    for r, payload in enumerate((below, own, above)):
        for t in range(held):
            table[r * span + t, 0:6] = payload[pl.ds(t, 6, stride=held)]
        table[r * span + held, 0:6] = payload[6 * held : 6 * held + 6]
        table[r * span + held + 1, 0:6] = payload[6 * held + 6 : 6 * held + 12]
    total[...] = jnp.zeros_like(total)

    def visit(step, carry):
        bonds(step).wait()
        gains = []
        for g in range(GROUP):
            k = step * GROUP + g
            slot_a, slot_b = info[0, k], info[1, k]
            mid_x = info[2, k].astype(jnp.float32) + 1.5
            mid_y = info[3, k].astype(jnp.float32) + 1.5
            gain_a, gain_b = pair_forces(
                table[slot_a], table[slot_b], mid_x, mid_y, held_bonds[k], mid_z
            )
            gains.append((slot_a, gain_a))
            gains.append((slot_b, gain_b))
        for slot, gain in gains:
            total[slot] += gain
        return carry

    lax.fori_loop(0, steps, visit, 0)

    for r, out in enumerate((down, force, up)):
        for t in range(held):
            out[pl.ds(t, 3, stride=held)] = total[r * span + t, 0:3]
    for r, out, at in ((0, down, 3 * held), (1, edges, 0), (2, up, 3 * held)):
        out[at : at + 3] = total[r * span + held, 0:3]
        out[at + 3 : at + 6] = total[r * span + held + 1, 0:3]
    for out in (down, up):
        end = 3 * span
        out[end:] = jnp.zeros((out.shape[0] - end, out.shape[1]), jnp.float32)


def merge_kernel(held, force, from_above, from_below, to_first, to_last, out):
    rows = 3 * held
    out[...] = force[...] + (from_above[0:rows] + from_below[0:rows])
    out[pl.ds(0, 3, stride=held)] += to_first[...]
    out[pl.ds(held - 1, 3, stride=held)] += to_last[...]


def limit(mebibytes):
    return pltpu.CompilerParams(vmem_limit_bytes=mebibytes * 1024 * 1024)


def bond_call(held, count, points):
    span = held + 2
    f32 = jnp.float32
    sent = jax.ShapeDtypeStruct((padded_rows(3 * span), points), f32)
    return pl.pallas_call(
        functools.partial(bond_kernel, 3.5, held),
        out_shape=(
            jax.ShapeDtypeStruct((3 * held, points), f32),
            sent,
            sent,
            jax.ShapeDtypeStruct((6, points), f32),
        ),
        in_specs=[SMEM] + [VMEM] * 3 + [HBM],
        out_specs=(VMEM,) * 4,
        scratch_shapes=[pltpu.VMEM((3 * span, 8, points), f32)] * 2
        + [
            pltpu.VMEM((count, points, points), jnp.int32),
            pltpu.SemaphoreType.DMA((count // GROUP,)),
        ],
        compiler_params=limit(8),
        name="bond_forces",
    )


def on_device(coords, displacement, pairs, intact):
    held, _, points = coords.shape
    span = held + 2
    strip_tiles = held * lax.axis_size("tile")
    f32 = jnp.float32

    edge = jax.ShapeDtypeStruct((6, points), f32)
    packed = jax.ShapeDtypeStruct((padded_rows(6 * span), points), f32)
    inside, first, last = pl.pallas_call(
        functools.partial(pack_kernel, held),
        out_shape=(packed, edge, edge),
        in_specs=[HBM] * 2,
        out_specs=(VMEM,) * 3,
        scratch_shapes=[pltpu.SemaphoreType.DMA((2,))],
        compiler_params=limit(1),
        name="pack_payload",
    )(
        in_hbm(jnp.transpose(coords, (1, 0, 2)).reshape(-1, points)),
        in_hbm(jnp.transpose(displacement, (1, 0, 2)).reshape(-1, points)),
    )
    left = shifted(last, "tile", 1)
    right = shifted(first, "tile", -1)
    own = pl.pallas_call(
        functools.partial(frame_kernel, held),
        out_shape=packed,
        in_specs=[VMEM] * 3,
        out_specs=VMEM,
        input_output_aliases={0: 0},
        compiler_params=limit(1),
        name="frame_payload",
    )(inside, left, right)
    below = shifted(own, "strip", 1)
    above = shifted(own, "strip", -1)

    strip_of, place = pairs // strip_tiles, pairs % strip_tiles
    row = strip_of - lax.axis_index("strip") + 1
    local = place - lax.axis_index("tile") * held
    column = jnp.where(local < 0, held, jnp.where(local >= held, held + 1, local))
    slots = row * span + column
    info = jnp.stack(
        [
            slots[:, 0],
            slots[:, 1],
            2 * (strip_of[:, 0] + strip_of[:, 1]),
            2 * (place[:, 0] + place[:, 1]),
        ]
    )
    force, down, up, edges = bond_call(held, intact.shape[0], points)(info, below, own, above, in_hbm(intact))
    from_above = shifted(down, "strip", -1)
    from_below = shifted(up, "strip", 1)
    tail = slice(3 * held, 3 * held + 6)
    edge = edges + (from_above[tail] + from_below[tail])
    to_last = shifted(edge[0:3], "tile", -1)
    to_first = shifted(edge[3:6], "tile", 1)
    merged = pl.pallas_call(
        functools.partial(merge_kernel, held),
        out_shape=jax.ShapeDtypeStruct((3 * held, points), f32),
        in_specs=[VMEM] * 5,
        out_specs=VMEM,
        compiler_params=limit(1),
        name="merge_forces",
    )(force, from_above, from_below, to_first, to_last)
    return jnp.transpose(merged.reshape(3, held, points), (1, 0, 2))


def solution(mesh):
    placed = P(("strip", "tile"), None, None)
    return jax.shard_map(
        on_device,
        mesh=mesh,
        in_specs=(placed, placed, P(("strip", "tile"), None), placed),
        out_specs=placed,
        check_vma=False,
    )
```

```python
import functools

import jax
import jax.numpy as jnp
from jax import lax
from jax.experimental import pallas as pl
from jax.experimental.pallas import tpu as pltpu
from jax.sharding import PartitionSpec as P

HORIZON = 3.0
STIFFNESS = 2.0
ONSET = 0.02
FINAL = 0.05

GROUP = 8
EDGES = 4
VMEM = pl.BlockSpec(memory_space=pltpu.VMEM)
HBM = pl.BlockSpec(memory_space=pltpu.HBM)
SMEM = pl.BlockSpec(memory_space=pltpu.SMEM)


def shifted(value, axis, step):
    count = lax.axis_size(axis)
    first, last = max(0, -step), min(count, count - step)
    return lax.ppermute(value, axis, [(i, i + step) for i in range(first, last)])


def in_hbm(value):
    return pltpu.with_memory_space_constraint(value, pltpu.HBM)


def padded_rows(rows):
    return (rows + 7) // 8 * 8


def pack_kernel(held, coords, displacement, out, edges, arrived):
    rows = 3 * held
    copies = [
        pltpu.make_async_copy(source, out.at[pl.ds(i * rows, rows)], arrived.at[i])
        for i, source in enumerate((coords, displacement))
    ]
    for copy in copies:
        copy.start()
    for copy in copies:
        copy.wait()
    for i, t in enumerate((0, held - 1)):
        edges[6 * i : 6 * i + 6] = out[pl.ds(t, 6, stride=held)]


def frame_kernel(held, payload, near, far, out):
    end = 6 * held
    out[end : end + 12] = near[...]
    out[end + 12 : end + 24] = far[...]


def stage_kernel(payload, bonds, out, arrived):
    copy = pltpu.make_async_copy(bonds, out, arrived)
    copy.start()
    copy.wait()


def pieces(value):
    first = value.astype(jnp.bfloat16).astype(jnp.float32)
    rest = value - first
    second = rest.astype(jnp.bfloat16).astype(jnp.float32)
    return first, second, rest - second


def middle_of(mid_x, mid_y, mid_z, points):
    row = lax.broadcasted_iota(jnp.int32, (8, points), 0)
    return jnp.where(
        row == 0, mid_x, jnp.where(row == 1, mid_y, jnp.where(row == 2, mid_z, 0.0))
    )


def side_rows(here, row):
    moved = pltpu.roll(here, 5, axis=0)
    now = here + moved
    low = row < 3
    square = jnp.sum(jnp.where(low, here * here, 0.0), axis=0, keepdims=True)
    growth = jnp.sum(jnp.where(low, moved * (here + now), 0.0), axis=0, keepdims=True)
    return moved, now, square, growth


def now_rows(now, row):
    first = now.astype(jnp.bfloat16).astype(jnp.float32)
    second = now - first
    top = jnp.where(row < 3, first, jnp.where(row == 3, 1.0, 0.0))
    rows = jnp.concatenate([top, jnp.where(row < 3, second, 0.0)], axis=0)
    rows = rows.astype(jnp.bfloat16)
    return jnp.concatenate([rows, rows], axis=1)


def pair_squares(here_a, here_b):
    points = here_a.shape[-1]
    row = lax.broadcasted_iota(jnp.int32, (8, points), 0)
    _, _, square_a, growth_a = side_rows(here_a, row)
    moved_b, now_b, square_b, growth_b = side_rows(here_b, row)

    six, seven = row == 6, row == 7
    left = jnp.where(row < 6, -2.0 * here_a, jnp.where(six, square_a, growth_a))
    l1, l2, l3 = pieces(left)

    def ones(value):
        return jnp.where(row < 6, value, jnp.where(six, 1.0, 0.0))

    o1, o2 = ones(l1), ones(l2)
    lhs = jnp.concatenate([l1, l2, l3, o1, o2, o1], axis=0).astype(jnp.bfloat16)

    shifted_b = pltpu.roll(now_b, 3, axis=0)
    right_ref = jnp.where(row < 3, here_b, jnp.where(six, square_b, 0.0))
    right_gain = jnp.where(
        row < 3, moved_b, jnp.where(row < 6, shifted_b, jnp.where(six, growth_b, 0.0))
    )

    def stack(value, at_six, at_seven):
        p1, p2, p3 = pieces(value)
        base = jnp.where(six, at_six, jnp.where(seven, at_seven, p1))
        mixed = jnp.where(six, p1, p2)
        return jnp.concatenate([base, base, base, mixed, p2, p3], axis=0)

    rhs = jnp.concatenate([stack(right_ref, 1.0, 0.0), stack(right_gain, 0.0, 1.0)], axis=1)
    return lax.dot_general(
        lhs, rhs.astype(jnp.bfloat16), (((0,), (0,)), ((), ())), preferred_element_type=jnp.float32
    )


def pull_of(both, bond_mask):
    points = bond_mask.shape[-1]
    ref2, gain2 = both[:, :points], both[:, points:]
    now2 = jnp.maximum(ref2 + gain2, 1e-7)
    per_ref, per_now = lax.rsqrt(ref2), lax.rsqrt(now2)
    length_ref, length_now = ref2 * per_ref, now2 * per_now
    stretch = (gain2 * per_ref) * (1.0 / (length_now + length_ref))
    influence = jnp.maximum(1.0 - length_ref, 0.0)
    soften = jnp.clip(FINAL - stretch, 0.0, FINAL - ONSET)
    pull = ((stretch * influence) * soften) * (per_now * bond_mask.astype(jnp.float32))
    high = pull.astype(jnp.bfloat16)
    low = (pull - high.astype(jnp.float32)).astype(jnp.bfloat16)
    return high, low


def gather_pair(now_a, now_b, high, low):
    row = lax.broadcasted_iota(jnp.int32, now_a.shape, 0)
    on_b = jnp.dot(
        now_rows(now_a, row),
        jnp.concatenate([high, low], axis=0),
        preferred_element_type=jnp.float32,
    )
    on_a = lax.dot_general(
        now_rows(now_b, row),
        jnp.concatenate([high, low], axis=1),
        (((1,), (1,)), ((), ())),
        preferred_element_type=jnp.float32,
    )
    sum_a, sum_b = on_a[0:8] + on_a[8:16], on_b[0:8] + on_b[8:16]
    scale = STIFFNESS / (FINAL - ONSET)
    return scale * (sum_a - now_a * sum_a[3:4]), scale * (sum_b - now_b * sum_b[3:4])


def bond_kernel(
    mid_z, held, info, below, own, above, bonds, force, down, up, edges,
    table, total, squares0, squares1, pulls0, pulls1
):
    count, points, _ = bonds.shape
    steps = count // GROUP
    span = held + EDGES
    for r, payload in enumerate((below, own, above)):
        for t in range(held):
            table[r * span + t, 0:6] = payload[pl.ds(t, 6, stride=held)]
        for i in range(EDGES):
            at = 6 * (held + i)
            table[r * span + held + i, 0:6] = payload[at : at + 6]
    total[...] = jnp.zeros_like(total)

    def ends(k):
        mid_x = info[2, k].astype(jnp.float32) + 1.5
        mid_y = info[3, k].astype(jnp.float32) + 1.5
        middle = middle_of(mid_x, mid_y, mid_z, points)
        return (table[info[0, k]] - middle) * (1.0 / HORIZON), (
            table[info[1, k]] - middle
        ) * (1.0 / HORIZON)

    def measure(step, squares):
        for g in range(GROUP):
            squares[g] = pair_squares(*ends(step * GROUP + g))

    def visit(step, squares, pulls):
        for g in range(GROUP):
            high, low = pull_of(squares[g], bonds[step * GROUP + g])
            pulls[g, 0:points], pulls[g, points:] = high, low

    def collect(step, pulls):
        gains = []
        for g in range(GROUP):
            k = step * GROUP + g
            here_a, here_b = ends(k)
            gain_a, gain_b = gather_pair(
                here_a + pltpu.roll(here_a, 5, axis=0),
                here_b + pltpu.roll(here_b, 5, axis=0),
                pulls[g, 0:points],
                pulls[g, points:],
            )
            gains.append((info[0, k], gain_a))
            gains.append((info[1, k], gain_b))
        for slot, gain in gains:
            total[slot] += gain

    measure(0, squares0)
    measure(1, squares1)
    visit(0, squares0, pulls0)

    @pl.loop(1, steps // 2)
    def _(twice):
        step = 2 * twice
        measure(step, squares0)
        visit(step - 1, squares1, pulls1)
        collect(step - 2, pulls0)
        measure(step + 1, squares1)
        visit(step, squares0, pulls0)
        collect(step - 1, pulls1)

    visit(steps - 1, squares1, pulls1)
    collect(steps - 2, pulls0)
    collect(steps - 1, pulls1)

    for r, out in enumerate((down, force, up)):
        for t in range(held):
            out[pl.ds(t, 3, stride=held)] = total[r * span + t, 0:3]
    for r, out, at in ((0, down, 3 * held), (1, edges, 0), (2, up, 3 * held)):
        for i in range(EDGES):
            out[at + 3 * i : at + 3 * i + 3] = total[r * span + held + i, 0:3]
    for out in (down, up):
        end = 3 * span
        if end < out.shape[0]:
            out[end:] = jnp.zeros((out.shape[0] - end, out.shape[1]), jnp.float32)


def merge_kernel(held, force, from_above, from_below, near, far, out):
    rows = 3 * held
    out[...] = force[...] + (from_above[0:rows] + from_below[0:rows])
    out[pl.ds(0, 3, stride=held)] += near[0:3] + far[0:3]
    out[pl.ds(held - 1, 3, stride=held)] += near[3:6] + far[3:6]


def limit(mebibytes):
    return pltpu.CompilerParams(vmem_limit_bytes=mebibytes * 1024 * 1024)


def bond_call(held, count, points):
    span = held + EDGES
    f32 = jnp.float32
    sent = jax.ShapeDtypeStruct((padded_rows(3 * span), points), f32)
    return pl.pallas_call(
        functools.partial(bond_kernel, 3.5, held),
        out_shape=(
            jax.ShapeDtypeStruct((3 * held, points), f32),
            sent,
            sent,
            jax.ShapeDtypeStruct((3 * EDGES, points), f32),
        ),
        in_specs=[SMEM] + [VMEM] * 4,
        out_specs=(VMEM,) * 4,
        scratch_shapes=[pltpu.VMEM((3 * span, 8, points), f32)] * 2
        + [pltpu.VMEM((GROUP, points, 2 * points), f32)] * 2
        + [pltpu.VMEM((GROUP, 2 * points, points), jnp.bfloat16)] * 2,
        compiler_params=limit(8),
        name="bond_forces",
    )


def swapped(value, axis, phase):
    pairs = []
    for i in range(phase, lax.axis_size(axis) - 1, 2):
        pairs += [(i, i + 1), (i + 1, i)]
    return lax.ppermute(value, axis, pairs)


def on_device(coords, displacement, pairs, intact):
    held, _, points = coords.shape
    span = held + EDGES
    strip_tiles = held * lax.axis_size("tile")
    f32 = jnp.float32

    packed = jax.ShapeDtypeStruct((padded_rows(6 * span), points), f32)
    inside, ends = pl.pallas_call(
        functools.partial(pack_kernel, held),
        out_shape=(packed, jax.ShapeDtypeStruct((12, points), f32)),
        in_specs=[HBM] * 2,
        out_specs=(VMEM,) * 2,
        scratch_shapes=[pltpu.SemaphoreType.DMA((2,))],
        compiler_params=limit(1),
        name="pack_payload",
    )(
        in_hbm(jnp.transpose(coords, (1, 0, 2)).reshape(-1, points)),
        in_hbm(jnp.transpose(displacement, (1, 0, 2)).reshape(-1, points)),
    )
    near = swapped(ends, "tile", 0)
    far = swapped(ends, "tile", 1)

    tile_index = lax.axis_index("tile")
    strip_of, place = pairs // strip_tiles, pairs % strip_tiles
    row = strip_of - lax.axis_index("strip") + 1
    local = place - tile_index * held
    odd = tile_index % 2
    column = jnp.where(
        local < 0, held + 3 - 2 * odd, jnp.where(local >= held, held + 2 * odd, local)
    )
    slots = row * span + column
    info = jnp.stack(
        [
            slots[:, 0],
            slots[:, 1],
            2 * (strip_of[:, 0] + strip_of[:, 1]),
            2 * (place[:, 0] + place[:, 1]),
        ]
    )

    own = pl.pallas_call(
        functools.partial(frame_kernel, held),
        out_shape=packed,
        in_specs=[VMEM] * 3,
        out_specs=VMEM,
        input_output_aliases={0: 0},
        compiler_params=limit(1),
        name="frame_payload",
    )(inside, near, far)
    below = shifted(own, "strip", 1)
    above = shifted(own, "strip", -1)
    bonds = pl.pallas_call(
        stage_kernel,
        out_shape=jax.ShapeDtypeStruct(intact.shape, intact.dtype),
        in_specs=[VMEM, HBM],
        out_specs=VMEM,
        scratch_shapes=[pltpu.SemaphoreType.DMA],
        compiler_params=limit(1),
        cost_estimate=pl.CostEstimate(
            flops=0, bytes_accessed=4 * intact.size, transcendentals=0
        ),
        name="stage_bonds",
    )(own, in_hbm(intact))

    force, down, up, edges = bond_call(held, intact.shape[0], points)(
        info, below, own, above, bonds
    )
    from_above = shifted(down, "strip", -1)
    from_below = shifted(up, "strip", 1)
    tail = slice(3 * held, 3 * span)
    edge = edges + (from_above[tail] + from_below[tail])
    near_force = swapped(edge[0:6], "tile", 0)
    far_force = swapped(edge[6:12], "tile", 1)
    merged = pl.pallas_call(
        functools.partial(merge_kernel, held),
        out_shape=jax.ShapeDtypeStruct((3 * held, points), f32),
        in_specs=[VMEM] * 5,
        out_specs=VMEM,
        compiler_params=limit(1),
        name="merge_forces",
    )(force, from_above, from_below, near_force, far_force)
    return jnp.transpose(merged.reshape(3, held, points), (1, 0, 2))


def solution(mesh):
    placed = P(("strip", "tile"), None, None)
    return jax.shard_map(
        on_device,
        mesh=mesh,
        in_specs=(placed, placed, P(("strip", "tile"), None), placed),
        out_specs=placed,
        check_vma=False,
    )
```

```python
import functools

import jax
import jax.numpy as jnp
from jax import lax
from jax.experimental import pallas as pl
from jax.experimental.pallas import tpu as pltpu
from jax.sharding import PartitionSpec as P

HORIZON = 3.0
STIFFNESS = 2.0
ONSET = 0.02
FINAL = 0.05

GROUP = 2
EDGES = 4
ROOM = 80
ABOVE, BELOW, SAME = 0, 1, 2
VMEM = pl.BlockSpec(memory_space=pltpu.VMEM)
HBM = pl.BlockSpec(memory_space=pltpu.HBM)
SMEM = pl.BlockSpec(memory_space=pltpu.SMEM)


def shifted(value, axis, step):
    count = lax.axis_size(axis)
    first, last = max(0, -step), min(count, count - step)
    return lax.ppermute(value, axis, [(i, i + step) for i in range(first, last)])


def in_hbm(value):
    return pltpu.with_memory_space_constraint(value, pltpu.HBM)


def padded_rows(rows):
    return (rows + 7) // 8 * 8


def pack_kernel(held, coords, displacement, out, edges, arrived):
    rows = 3 * held
    copies = [
        pltpu.make_async_copy(source, out.at[pl.ds(i * rows, rows)], arrived.at[i])
        for i, source in enumerate((coords, displacement))
    ]
    for copy in copies:
        copy.start()
    for copy in copies:
        copy.wait()
    for i, t in enumerate((0, held - 1)):
        edges[6 * i : 6 * i + 6] = out[pl.ds(t, 6, stride=held)]


def frame_kernel(held, payload, near, far, out):
    end = 6 * held
    out[end : end + 12] = near[...]
    out[end + 12 : end + 24] = far[...]


def stage_kernel(held, strip_tiles, payload, pairs, intact, bonds, info, arrived):
    copy = pltpu.make_async_copy(intact, bonds, arrived)
    copy.start()
    device = lax.div(pairs[0, 0], held)
    base = device * held
    strip = lax.div(base, strip_tiles)
    start = base - strip * strip_tiles
    odd = device % 2

    def place(k, counts):
        first, second = pairs[0, k] - base, pairs[1, k] - base
        half = strip_tiles // 2
        side = jnp.where(second > half, 1, jnp.where(second < -half, -1, 0))
        local = second - side * strip_tiles
        column = jnp.where(
            local < 0, held + 3 - 2 * odd, jnp.where(local >= held, held + 2 * odd, local)
        )
        above, below, same = counts
        at = jnp.where(
            side > 0,
            ABOVE * ROOM + above,
            jnp.where(side < 0, BELOW * ROOM + below, SAME * ROOM + same),
        )
        info[0, at] = first
        info[1, at] = column
        info[2, at] = 2 * (2 * strip + side)
        info[3, at] = 2 * (2 * start + first + local)
        info[4, at] = k
        up, down = jnp.where(side > 0, 1, 0), jnp.where(side < 0, 1, 0)
        return above + up, below + down, same + (1 - up - down)

    zero = jnp.int32(0)
    counts = lax.fori_loop(0, pairs.shape[1], place, (zero, zero, zero), unroll=4)
    for kind, count in enumerate(counts):
        info[5, kind] = count
        for i in range(2 * GROUP):
            at = kind * ROOM + count + i
            info[0, at], info[1, at] = held, held + EDGES
            for field in (2, 3, 4):
                info[field, at] = 0
    copy.wait()


def pieces(value):
    first = value.astype(jnp.bfloat16).astype(jnp.float32)
    rest = value - first
    second = rest.astype(jnp.bfloat16).astype(jnp.float32)
    return first, second, rest - second


def middle_of(mid_x, mid_y, mid_z, points):
    row = lax.broadcasted_iota(jnp.int32, (8, points), 0)
    return jnp.where(
        row == 0, mid_x, jnp.where(row == 1, mid_y, jnp.where(row == 2, mid_z, 0.0))
    )


def side_rows(here, row):
    moved = pltpu.roll(here, 5, axis=0)
    now = here + moved
    low = row < 3
    square = jnp.sum(jnp.where(low, here * here, 0.0), axis=0, keepdims=True)
    growth = jnp.sum(jnp.where(low, moved * (here + now), 0.0), axis=0, keepdims=True)
    return moved, now, square, growth


def now_rows(now, row):
    first = now.astype(jnp.bfloat16).astype(jnp.float32)
    second = now - first
    top = jnp.where(row < 3, first, jnp.where(row == 3, 1.0, 0.0))
    rows = jnp.concatenate([top, jnp.where(row < 3, second, 0.0)], axis=0)
    rows = rows.astype(jnp.bfloat16)
    return jnp.concatenate([rows, rows], axis=1)


def pair_squares(here_a, here_b):
    points = here_a.shape[-1]
    row = lax.broadcasted_iota(jnp.int32, (8, points), 0)
    _, _, square_a, growth_a = side_rows(here_a, row)
    moved_b, now_b, square_b, growth_b = side_rows(here_b, row)

    six, seven = row == 6, row == 7
    left = jnp.where(row < 6, -2.0 * here_a, jnp.where(six, square_a, growth_a))
    l1, l2, l3 = pieces(left)

    def ones(value):
        return jnp.where(row < 6, value, jnp.where(six, 1.0, 0.0))

    o1, o2 = ones(l1), ones(l2)
    lhs = jnp.concatenate([l1, l2, l3, o1, o2, o1], axis=0).astype(jnp.bfloat16)

    shifted_b = pltpu.roll(now_b, 3, axis=0)
    right_ref = jnp.where(row < 3, here_b, jnp.where(six, square_b, 0.0))
    right_gain = jnp.where(
        row < 3, moved_b, jnp.where(row < 6, shifted_b, jnp.where(six, growth_b, 0.0))
    )

    def stack(value, at_six, at_seven):
        p1, p2, p3 = pieces(value)
        base = jnp.where(six, at_six, jnp.where(seven, at_seven, p1))
        mixed = jnp.where(six, p1, p2)
        return jnp.concatenate([base, base, base, mixed, p2, p3], axis=0)

    rhs = jnp.concatenate([stack(right_ref, 1.0, 0.0), stack(right_gain, 0.0, 1.0)], axis=1)
    return lax.dot_general(
        lhs, rhs.astype(jnp.bfloat16), (((0,), (0,)), ((), ())), preferred_element_type=jnp.float32
    )


def pull_of(both, bond_mask):
    points = bond_mask.shape[-1]
    ref2, gain2 = both[:, :points], both[:, points:]
    now2 = jnp.maximum(ref2 + gain2, 1e-7)
    per_ref, per_now = lax.rsqrt(ref2), lax.rsqrt(now2)
    length_ref, length_now = ref2 * per_ref, now2 * per_now
    stretch = (gain2 * per_ref) * (1.0 / (length_now + length_ref))
    influence = jnp.maximum(1.0 - length_ref, 0.0)
    soften = jnp.clip(FINAL - stretch, 0.0, FINAL - ONSET)
    pull = ((stretch * influence) * soften) * (per_now * bond_mask.astype(jnp.float32))
    high = pull.astype(jnp.bfloat16)
    low = (pull - high.astype(jnp.float32)).astype(jnp.bfloat16)
    return high, low


def gather_pair(now_a, now_b, high, low):
    row = lax.broadcasted_iota(jnp.int32, now_a.shape, 0)
    on_b = jnp.dot(
        now_rows(now_a, row),
        jnp.concatenate([high, low], axis=0),
        preferred_element_type=jnp.float32,
    )
    on_a = lax.dot_general(
        now_rows(now_b, row),
        jnp.concatenate([high, low], axis=1),
        (((1,), (1,)), ((), ())),
        preferred_element_type=jnp.float32,
    )
    sum_a, sum_b = on_a[0:8] + on_a[8:16], on_b[0:8] + on_b[8:16]
    scale = STIFFNESS / (FINAL - ONSET)
    return scale * (sum_a - now_a * sum_a[3:4]), scale * (sum_b - now_b * sum_b[3:4])


def sum_bonds(
    kind, mid_z, held, info, own, other, bonds,
    first_table, second_table, first_total, second_total,
    squares0, squares1, pulls0, pulls1
):
    points = bonds.shape[-1]
    for t in range(held):
        first_table[t, 0:6] = own[pl.ds(t, 6, stride=held)]
        second_table[t, 0:6] = other[pl.ds(t, 6, stride=held)]
    for i in range(EDGES):
        at = 6 * (held + i)
        second_table[held + i, 0:6] = other[at : at + 6]
    first_total[...] = jnp.zeros_like(first_total)
    second_total[...] = jnp.zeros_like(second_total)
    pairs_a_turn = 2 * GROUP
    turns = jnp.maximum(lax.div(info[5, kind] + (pairs_a_turn - 1), pairs_a_turn), 1)
    steps = 2 * turns

    def ends(k):
        mid_x = info[2, k].astype(jnp.float32) + 1.5
        mid_y = info[3, k].astype(jnp.float32) + 1.5
        middle = middle_of(mid_x, mid_y, mid_z, points)
        return (first_table[info[0, k]] - middle) * (1.0 / HORIZON), (
            second_table[info[1, k]] - middle
        ) * (1.0 / HORIZON)

    def members(step):
        return [kind * ROOM + step * GROUP + g for g in range(GROUP)]

    def measure(step, squares):
        for g, k in enumerate(members(step)):
            squares[g] = pair_squares(*ends(k))

    def visit(step, squares, pulls):
        for g, k in enumerate(members(step)):
            high, low = pull_of(squares[g], bonds[info[4, k]])
            pulls[g, 0:points], pulls[g, points:] = high, low

    def collect(step, pulls):
        gains = []
        for g, k in enumerate(members(step)):
            here_a, here_b = ends(k)
            gain_a, gain_b = gather_pair(
                here_a + pltpu.roll(here_a, 5, axis=0),
                here_b + pltpu.roll(here_b, 5, axis=0),
                pulls[g, 0:points],
                pulls[g, points:],
            )
            gains.append((info[0, k], gain_a, info[1, k], gain_b))
        for slot_a, gain_a, slot_b, gain_b in gains:
            first_total[slot_a] += gain_a
            second_total[slot_b] += gain_b

    measure(0, squares0)
    measure(1, squares1)
    visit(0, squares0, pulls0)

    @pl.loop(1, turns)
    def _(twice):
        step = 2 * twice
        measure(step, squares0)
        visit(step - 1, squares1, pulls1)
        collect(step - 2, pulls0)
        measure(step + 1, squares1)
        visit(step, squares0, pulls0)
        collect(step - 1, pulls1)

    visit(steps - 1, squares1, pulls1)
    collect(steps - 2, pulls0)
    collect(steps - 1, pulls1)


def across_kernel(kind, mid_z, held, info, own, other, bonds, before, force, sent, *scratch):
    sum_bonds(kind, mid_z, held, info, own, other, bonds, *scratch)
    first_total, second_total = scratch[2:4]
    for t in range(held):
        force[pl.ds(t, 3, stride=held)] = first_total[t, 0:3]
        sent[pl.ds(t, 3, stride=held)] = second_total[t, 0:3]
    for i in range(EDGES):
        at = 3 * (held + i)
        sent[at : at + 3] = second_total[held + i, 0:3]
    end = 3 * (held + EDGES)
    if end < sent.shape[0]:
        sent[end:] = jnp.zeros((sent.shape[0] - end, sent.shape[1]), jnp.float32)
    if before is not None:
        force[...] += before[...]


def first_across_kernel(kind, mid_z, held, info, own, other, bonds, *rest):
    across_kernel(kind, mid_z, held, info, own, other, bonds, None, *rest)


def within_kernel(mid_z, held, info, own, bonds, before, from_below, force, edges, *scratch):
    sum_bonds(SAME, mid_z, held, info, own, own, bonds, *scratch)
    first_total, second_total = scratch[2:4]
    for t in range(held):
        force[pl.ds(t, 3, stride=held)] = first_total[t, 0:3] + second_total[t, 0:3]
    for i in range(EDGES):
        edges[3 * i : 3 * i + 3] = second_total[held + i, 0:3]
    rows = 3 * held
    force[...] += before[...] + from_below[0:rows]
    edges[...] += from_below[rows : rows + 3 * EDGES]


def merge_kernel(held, force, from_above, near, far, out):
    rows = 3 * held
    out[...] = force[...] + from_above[0:rows]
    out[pl.ds(0, 3, stride=held)] += near[0:3] + far[0:3]
    out[pl.ds(held - 1, 3, stride=held)] += near[3:6] + far[3:6]


def limit(mebibytes):
    return pltpu.CompilerParams(vmem_limit_bytes=mebibytes * 1024 * 1024)


MID_Z = 3.5


def bond_call(kernel, held, points, inputs, last_rows, name, megabytes):
    span = held + EDGES
    f32 = jnp.float32
    return pl.pallas_call(
        kernel,
        out_shape=(
            jax.ShapeDtypeStruct((3 * held, points), f32),
            jax.ShapeDtypeStruct((last_rows, points), f32),
        ),
        in_specs=[SMEM] + [VMEM] * inputs,
        out_specs=(VMEM, VMEM),
        scratch_shapes=[
            pltpu.VMEM((held + 1, 8, points), f32),
            pltpu.VMEM((span + 1, 8, points), f32),
            pltpu.VMEM((held + 1, 8, points), f32),
            pltpu.VMEM((span + 1, 8, points), f32),
        ]
        + [pltpu.VMEM((GROUP, points, 2 * points), f32)] * 2
        + [pltpu.VMEM((GROUP, 2 * points, points), jnp.bfloat16)] * 2,
        compiler_params=limit(4),
        cost_estimate=pl.CostEstimate(
            flops=0, bytes_accessed=megabytes << 20, transcendentals=0
        ),
        name=name,
    )


def stage_call(held, strip_tiles, intact):
    return pl.pallas_call(
        functools.partial(stage_kernel, held, strip_tiles),
        out_shape=(
            jax.ShapeDtypeStruct(intact.shape, intact.dtype),
            jax.ShapeDtypeStruct((6, 256), jnp.int32),
        ),
        in_specs=[VMEM, SMEM, HBM],
        out_specs=(VMEM, SMEM),
        scratch_shapes=[pltpu.SemaphoreType.DMA],
        compiler_params=limit(1),
        cost_estimate=pl.CostEstimate(
            flops=0, bytes_accessed=4 * intact.size, transcendentals=0
        ),
        name="stage_bonds",
    )


def bond_sums(held, points, info, own, below, above, bonds, send_up, send_down):
    sent_rows = padded_rows(3 * (held + EDGES))
    force, up = bond_call(
        functools.partial(first_across_kernel, ABOVE, MID_Z, held),
        held, points, 3, sent_rows, "bonds_above", 8,
    )(info, own, above, bonds)
    from_below = send_up(up)
    force, down = bond_call(
        functools.partial(across_kernel, BELOW, MID_Z, held),
        held, points, 4, sent_rows, "bonds_below", 8,
    )(info, own, below, bonds, force)
    from_above = send_down(down)
    force, edges = bond_call(
        functools.partial(within_kernel, MID_Z, held),
        held, points, 4, 3 * EDGES, "bonds_within", 8,
    )(info, own, bonds, force, from_below)
    return force, edges, from_above


def swapped(value, axis, phase):
    pairs = []
    for i in range(phase, lax.axis_size(axis) - 1, 2):
        pairs += [(i, i + 1), (i + 1, i)]
    return lax.ppermute(value, axis, pairs)


def on_device(coords, displacement, pairs, intact):
    held, _, points = coords.shape
    span = held + EDGES
    strip_tiles = held * lax.axis_size("tile")
    f32 = jnp.float32

    packed = jax.ShapeDtypeStruct((padded_rows(6 * span), points), f32)
    inside, ends = pl.pallas_call(
        functools.partial(pack_kernel, held),
        out_shape=(packed, jax.ShapeDtypeStruct((12, points), f32)),
        in_specs=[HBM] * 2,
        out_specs=(VMEM,) * 2,
        scratch_shapes=[pltpu.SemaphoreType.DMA((2,))],
        compiler_params=limit(1),
        name="pack_payload",
    )(
        in_hbm(jnp.transpose(coords, (1, 0, 2)).reshape(-1, points)),
        in_hbm(jnp.transpose(displacement, (1, 0, 2)).reshape(-1, points)),
    )
    near = swapped(ends, "tile", 0)
    far = swapped(ends, "tile", 1)

    own = pl.pallas_call(
        functools.partial(frame_kernel, held),
        out_shape=packed,
        in_specs=[VMEM] * 3,
        out_specs=VMEM,
        input_output_aliases={0: 0},
        compiler_params=limit(1),
        name="frame_payload",
    )(inside, near, far)
    below = shifted(own, "strip", 1)
    above = shifted(own, "strip", -1)
    bonds, info = stage_call(held, strip_tiles, intact)(
        own, jnp.transpose(pairs), in_hbm(intact)
    )
    force, edges, from_above = bond_sums(
        held,
        points,
        info,
        own,
        below,
        above,
        bonds,
        lambda up: shifted(up, "strip", 1),
        lambda down: shifted(down, "strip", -1),
    )
    tail = slice(3 * held, 3 * span)
    edge = edges + from_above[tail]
    near_force = swapped(edge[0:6], "tile", 0)
    far_force = swapped(edge[6:12], "tile", 1)
    merged = pl.pallas_call(
        functools.partial(merge_kernel, held),
        out_shape=jax.ShapeDtypeStruct((3 * held, points), f32),
        in_specs=[VMEM] * 4,
        out_specs=VMEM,
        compiler_params=limit(1),
        name="merge_forces",
    )(force, from_above, near_force, far_force)
    return jnp.transpose(merged.reshape(3, held, points), (1, 0, 2))


def solution(mesh):
    placed = P(("strip", "tile"), None, None)
    return jax.shard_map(
        on_device,
        mesh=mesh,
        in_specs=(placed, placed, P(("strip", "tile"), None), placed),
        out_specs=placed,
        check_vma=False,
    )
```

```python
import functools

import jax
import jax.numpy as jnp
from jax import lax
from jax.experimental import pallas as pl
from jax.experimental.pallas import tpu as pltpu
from jax.sharding import PartitionSpec as P

HORIZON = 3.0
STIFFNESS = 2.0
ONSET = 0.02
FINAL = 0.05

GROUP = 8
LEFT_GROUP = 8
MID_Z = 3.5
EDGES = 4
ALIGNED = 8
VMEM = pl.BlockSpec(memory_space=pltpu.VMEM)
HBM = pl.BlockSpec(memory_space=pltpu.HBM)
SMEM = pl.BlockSpec(memory_space=pltpu.SMEM)


def shifted(value, axis, step):
    count = lax.axis_size(axis)
    first, last = max(0, -step), min(count, count - step)
    return lax.ppermute(value, axis, [(i, i + step) for i in range(first, last)])


def in_hbm(value):
    return pltpu.with_memory_space_constraint(value, pltpu.HBM)


def padded_rows(rows):
    return (rows + 7) // 8 * 8


def ends_kernel(coords, displacement, ends, near_ends, arrived):
    held = coords.shape[1]
    copies = []
    for i, source in enumerate((coords, displacement)):
        for j, start in enumerate((0, held - ALIGNED)):
            copies.append(
                pltpu.make_async_copy(
                    source.at[:, pl.ds(start, ALIGNED), :],
                    near_ends.at[i, j],
                    arrived.at[2 * i + j],
                )
            )
    for copy in copies:
        copy.start()
    for copy in copies:
        copy.wait()
    for j, row in enumerate((0, ALIGNED - 1)):
        for i in range(2):
            for c in range(3):
                at = 6 * j + 3 * i + c
                ends[at : at + 1] = near_ends[i, j, c, row : row + 1]


def pack_kernel(held, coords, displacement, out, arrived):
    rows = 3 * held
    copies = [
        pltpu.make_async_copy(source, out.at[pl.ds(i * rows, rows)], arrived.at[i])
        for i, source in enumerate((coords, displacement))
    ]
    for copy in copies:
        copy.start()
    for copy in copies:
        copy.wait()


def frame_kernel(held, payload, near, far, out):
    end = 6 * held
    out[end : end + 12] = near[...]
    out[end + 12 : end + 24] = far[...]


def stage_kernel(held, info, own, bonds, out, left, table, arrived):
    copy = pltpu.make_async_copy(bonds, out, arrived)
    copy.start()
    base = held + EDGES
    for t in range(held):
        table[t, 0:6] = own[pl.ds(t, 6, stride=held)]

    @pl.loop(0, out.shape[0] // LEFT_GROUP)
    def _(step):
        for g in range(LEFT_GROUP):
            k = step * LEFT_GROUP + g
            here = centred(table[info[0, k] - base], info, k)
            left[k] = jnp.transpose(left_rows(here)).astype(jnp.bfloat16)

    copy.wait()


def pieces(value):
    first = value.astype(jnp.bfloat16).astype(jnp.float32)
    rest = value - first
    second = rest.astype(jnp.bfloat16).astype(jnp.float32)
    return first, second, rest - second


def middle_of(mid_x, mid_y, mid_z, points):
    row = lax.broadcasted_iota(jnp.int32, (8, points), 0)
    return jnp.where(
        row == 0, mid_x, jnp.where(row == 1, mid_y, jnp.where(row == 2, mid_z, 0.0))
    )


def centred(tile, info, k):
    mid_x = info[2, k].astype(jnp.float32) + 1.5
    mid_y = info[3, k].astype(jnp.float32) + 1.5
    return (tile - middle_of(mid_x, mid_y, MID_Z, tile.shape[-1])) * (1.0 / HORIZON)


def side_rows(here, row):
    moved = pltpu.roll(here, 5, axis=0)
    now = here + moved
    low = row < 3
    square = jnp.sum(jnp.where(low, here * here, 0.0), axis=0, keepdims=True)
    growth = jnp.sum(jnp.where(low, moved * (here + now), 0.0), axis=0, keepdims=True)
    return moved, now, square, growth


def now_rows(now, row):
    first = now.astype(jnp.bfloat16).astype(jnp.float32)
    second = now - first
    top = jnp.where(row < 3, first, jnp.where(row == 3, 1.0, 0.0))
    rows = jnp.concatenate([top, jnp.where(row < 3, second, 0.0)], axis=0)
    rows = rows.astype(jnp.bfloat16)
    return jnp.concatenate([rows, rows], axis=1)


def left_rows(here):
    row = lax.broadcasted_iota(jnp.int32, here.shape, 0)
    six = row == 6
    _, _, square, growth = side_rows(here, row)
    l1, l2, l3 = pieces(jnp.where(row < 6, -2.0 * here, jnp.where(six, square, growth)))

    def ones(value):
        return jnp.where(row < 6, value, jnp.where(six, 1.0, 0.0))

    o1, o2 = ones(l1), ones(l2)
    return jnp.concatenate([l1, l2, l3, o1, o2, o1], axis=0)


def right_rows(here):
    row = lax.broadcasted_iota(jnp.int32, here.shape, 0)
    six, seven = row == 6, row == 7
    moved, now, square, growth = side_rows(here, row)
    lowered = pltpu.roll(now, 3, axis=0)
    right_ref = jnp.where(row < 3, here, jnp.where(six, square, 0.0))
    right_gain = jnp.where(
        row < 3, moved, jnp.where(row < 6, lowered, jnp.where(six, growth, 0.0))
    )

    def stack(value, at_six, at_seven):
        p1, p2, p3 = pieces(value)
        base = jnp.where(six, at_six, jnp.where(seven, at_seven, p1))
        mixed = jnp.where(six, p1, p2)
        return jnp.concatenate([base, base, base, mixed, p2, p3], axis=0)

    return jnp.concatenate([stack(right_ref, 1.0, 0.0), stack(right_gain, 0.0, 1.0)], axis=1)


def pull_of(both, bond_mask):
    points = bond_mask.shape[-1]
    ref2, gain2 = both[:, :points], both[:, points:]
    now2 = jnp.maximum(ref2 + gain2, 1e-7)
    per_ref, per_now = lax.rsqrt(ref2), lax.rsqrt(now2)
    length_ref, length_now = ref2 * per_ref, now2 * per_now
    stretch = (gain2 * per_ref) * (1.0 / (length_now + length_ref))
    influence = jnp.maximum(1.0 - length_ref, 0.0)
    soften = jnp.clip(FINAL - stretch, 0.0, FINAL - ONSET)
    pull = ((stretch * influence) * soften) * (per_now * bond_mask.astype(jnp.float32))
    high = pull.astype(jnp.bfloat16)
    low = (pull - high.astype(jnp.float32)).astype(jnp.bfloat16)
    return high, low


def gather_pair(now_a, now_b, high, low):
    row = lax.broadcasted_iota(jnp.int32, now_a.shape, 0)
    on_b = jnp.dot(
        now_rows(now_a, row),
        jnp.concatenate([high, low], axis=0),
        preferred_element_type=jnp.float32,
    )
    on_a = lax.dot_general(
        now_rows(now_b, row),
        jnp.concatenate([high, low], axis=1),
        (((1,), (1,)), ((), ())),
        preferred_element_type=jnp.float32,
    )
    sum_a, sum_b = on_a[0:8] + on_a[8:16], on_b[0:8] + on_b[8:16]
    scale = STIFFNESS / (FINAL - ONSET)
    return scale * (sum_a - now_a * sum_a[3:4]), scale * (sum_b - now_b * sum_b[3:4])


def bond_kernel(
    held, info, below, own, above, bonds, left, force, down, up, edges,
    table, total, squares0, squares1, pulls0, pulls1
):
    count, points, _ = bonds.shape
    steps = count // GROUP
    span = held + EDGES
    for r, payload in enumerate((below, own, above)):
        for t in range(held):
            table[r * span + t, 0:6] = payload[pl.ds(t, 6, stride=held)]
        for i in range(EDGES):
            at = 6 * (held + i)
            table[r * span + held + i, 0:6] = payload[at : at + 6]
    total[...] = jnp.zeros_like(total)

    def measure(step, squares):
        for g in range(GROUP):
            k = step * GROUP + g
            rows = right_rows(centred(table[info[1, k]], info, k)).astype(jnp.bfloat16)
            squares[g] = jnp.dot(left[k], rows, preferred_element_type=jnp.float32)

    def visit(step, squares, pulls):
        for g in range(GROUP):
            high, low = pull_of(squares[g], bonds[step * GROUP + g])
            pulls[g, 0:points], pulls[g, points:] = high, low

    def collect(step, pulls):
        gains = []
        for g in range(GROUP):
            k = step * GROUP + g
            here_a, here_b = centred(table[info[0, k]], info, k), centred(table[info[1, k]], info, k)
            gain_a, gain_b = gather_pair(
                here_a + pltpu.roll(here_a, 5, axis=0),
                here_b + pltpu.roll(here_b, 5, axis=0),
                pulls[g, 0:points],
                pulls[g, points:],
            )
            gains.append((info[0, k], gain_a))
            gains.append((info[1, k], gain_b))
        for slot, gain in gains:
            total[slot] += gain

    measure(0, squares0)
    measure(1, squares1)
    visit(0, squares0, pulls0)

    @pl.loop(1, steps // 2)
    def _(twice):
        step = 2 * twice
        measure(step, squares0)
        visit(step - 1, squares1, pulls1)
        collect(step - 2, pulls0)
        measure(step + 1, squares1)
        visit(step, squares0, pulls0)
        collect(step - 1, pulls1)

    visit(steps - 1, squares1, pulls1)
    collect(steps - 2, pulls0)
    collect(steps - 1, pulls1)

    for r, out in enumerate((down, force, up)):
        for t in range(held):
            out[pl.ds(t, 3, stride=held)] = total[r * span + t, 0:3]
    for r, out, at in ((0, down, 3 * held), (1, edges, 0), (2, up, 3 * held)):
        for i in range(EDGES):
            out[at + 3 * i : at + 3 * i + 3] = total[r * span + held + i, 0:3]
    for out in (down, up):
        end = 3 * span
        if end < out.shape[0]:
            out[end:] = jnp.zeros((out.shape[0] - end, out.shape[1]), jnp.float32)


def merge_kernel(held, force, from_above, from_below, near, far, out):
    rows = 3 * held
    out[...] = force[...] + (from_above[0:rows] + from_below[0:rows])
    out[pl.ds(0, 3, stride=held)] += near[0:3] + far[0:3]
    out[pl.ds(held - 1, 3, stride=held)] += near[3:6] + far[3:6]


def limit(mebibytes):
    return pltpu.CompilerParams(vmem_limit_bytes=mebibytes * 1024 * 1024)


def stage_call(held, intact):
    count, points, _ = intact.shape
    return pl.pallas_call(
        functools.partial(stage_kernel, held),
        out_shape=(
            jax.ShapeDtypeStruct(intact.shape, intact.dtype),
            jax.ShapeDtypeStruct((count, points, 48), jnp.bfloat16),
        ),
        in_specs=[SMEM, VMEM, HBM],
        out_specs=(VMEM, VMEM),
        scratch_shapes=[
            pltpu.VMEM((held, 8, points), jnp.float32),
            pltpu.SemaphoreType.DMA,
        ],
        compiler_params=limit(2),
        cost_estimate=pl.CostEstimate(
            flops=0, bytes_accessed=4 * intact.size, transcendentals=0
        ),
        name="stage_bonds",
    )


def bond_call(held, count, points):
    span = held + EDGES
    f32 = jnp.float32
    sent = jax.ShapeDtypeStruct((padded_rows(3 * span), points), f32)
    return pl.pallas_call(
        functools.partial(bond_kernel, held),
        out_shape=(
            jax.ShapeDtypeStruct((3 * held, points), f32),
            sent,
            sent,
            jax.ShapeDtypeStruct((3 * EDGES, points), f32),
        ),
        in_specs=[SMEM] + [VMEM] * 5,
        out_specs=(VMEM,) * 4,
        scratch_shapes=[pltpu.VMEM((3 * span, 8, points), f32)] * 2
        + [pltpu.VMEM((GROUP, points, 2 * points), f32)] * 2
        + [pltpu.VMEM((GROUP, 2 * points, points), jnp.bfloat16)] * 2,
        compiler_params=limit(8),
        name="bond_forces",
    )


def swapped(value, axis, phase):
    pairs = []
    for i in range(phase, lax.axis_size(axis) - 1, 2):
        pairs += [(i, i + 1), (i + 1, i)]
    return lax.ppermute(value, axis, pairs)


def on_device(coords, displacement, pairs, intact):
    held, _, points = coords.shape
    span = held + EDGES
    strip_tiles = held * lax.axis_size("tile")
    f32 = jnp.float32

    packed = jax.ShapeDtypeStruct((padded_rows(6 * span), points), f32)
    places, shifts = jnp.transpose(coords, (1, 0, 2)), jnp.transpose(displacement, (1, 0, 2))
    ends = pl.pallas_call(
        ends_kernel,
        out_shape=jax.ShapeDtypeStruct((12, points), f32),
        in_specs=[HBM] * 2,
        out_specs=VMEM,
        scratch_shapes=[
            pltpu.VMEM((2, 2, 3, ALIGNED, points), f32),
            pltpu.SemaphoreType.DMA((4,)),
        ],
        compiler_params=limit(1),
        name="end_tiles",
    )(in_hbm(places), in_hbm(shifts))
    inside = pl.pallas_call(
        functools.partial(pack_kernel, held),
        out_shape=packed,
        in_specs=[HBM] * 2,
        out_specs=VMEM,
        scratch_shapes=[pltpu.SemaphoreType.DMA((2,))],
        compiler_params=limit(1),
        cost_estimate=pl.CostEstimate(flops=0, bytes_accessed=4 << 20, transcendentals=0),
        name="pack_payload",
    )(in_hbm(places.reshape(-1, points)), in_hbm(shifts.reshape(-1, points)))
    near = swapped(ends, "tile", 0)
    far = swapped(ends, "tile", 1)

    own = pl.pallas_call(
        functools.partial(frame_kernel, held),
        out_shape=packed,
        in_specs=[VMEM] * 3,
        out_specs=VMEM,
        input_output_aliases={0: 0},
        compiler_params=limit(1),
        name="frame_payload",
    )(inside, near, far)
    below = shifted(own, "strip", 1)
    above = shifted(own, "strip", -1)
    own, pairs = lax.optimization_barrier((own, pairs))
    tile_index = lax.axis_index("tile")
    strip_of, place = pairs // strip_tiles, pairs % strip_tiles
    row = strip_of - lax.axis_index("strip") + 1
    local = place - tile_index * held
    odd = tile_index % 2
    column = jnp.where(
        local < 0, held + 3 - 2 * odd, jnp.where(local >= held, held + 2 * odd, local)
    )
    slots = row * span + column
    info = jnp.stack(
        [
            slots[:, 0],
            slots[:, 1],
            2 * (strip_of[:, 0] + strip_of[:, 1]),
            2 * (place[:, 0] + place[:, 1]),
        ]
    )

    bonds, left = stage_call(held, intact)(info, own, in_hbm(intact))
    force, down, up, edges = bond_call(held, intact.shape[0], points)(
        info, below, own, above, bonds, left
    )
    from_above = shifted(down, "strip", -1)
    from_below = shifted(up, "strip", 1)
    tail = slice(3 * held, 3 * span)
    edge = edges + (from_above[tail] + from_below[tail])
    near_force = swapped(edge[0:6], "tile", 0)
    far_force = swapped(edge[6:12], "tile", 1)
    merged = pl.pallas_call(
        functools.partial(merge_kernel, held),
        out_shape=jax.ShapeDtypeStruct((3 * held, points), f32),
        in_specs=[VMEM] * 5,
        out_specs=VMEM,
        compiler_params=limit(1),
        name="merge_forces",
    )(force, from_above, from_below, near_force, far_force)
    return jnp.transpose(merged.reshape(3, held, points), (1, 0, 2))


def solution(mesh):
    placed = P(("strip", "tile"), None, None)
    return jax.shard_map(
        on_device,
        mesh=mesh,
        in_specs=(placed, placed, P(("strip", "tile"), None), placed),
        out_specs=placed,
        check_vma=False,
    )
```

```python
import functools

import jax
import jax.numpy as jnp
from jax import lax
from jax.experimental import pallas as pl
from jax.experimental.pallas import tpu as pltpu
from jax.sharding import PartitionSpec as P

HORIZON = 3.0
STIFFNESS = 2.0
ONSET = 0.02
FINAL = 0.05

GROUP = 64
LAG = 3
RING = 6
LEFT_GROUP = 8
MID_Z = 3.5
EDGES = 4
ALIGNED = 8
VMEM = pl.BlockSpec(memory_space=pltpu.VMEM)
HBM = pl.BlockSpec(memory_space=pltpu.HBM)
SMEM = pl.BlockSpec(memory_space=pltpu.SMEM)


def shifted(value, axis, step):
    count = lax.axis_size(axis)
    first, last = max(0, -step), min(count, count - step)
    return lax.ppermute(value, axis, [(i, i + step) for i in range(first, last)])


def in_hbm(value):
    return pltpu.with_memory_space_constraint(value, pltpu.HBM)


def padded_rows(rows):
    return (rows + 7) // 8 * 8


def ends_kernel(coords, displacement, ends, near_ends, arrived):
    held = coords.shape[1]
    copies = []
    for i, source in enumerate((coords, displacement)):
        for j, start in enumerate((0, held - ALIGNED)):
            copies.append(
                pltpu.make_async_copy(
                    source.at[:, pl.ds(start, ALIGNED), :],
                    near_ends.at[i, j],
                    arrived.at[2 * i + j],
                )
            )
    for copy in copies:
        copy.start()
    for copy in copies:
        copy.wait()
    for j, row in enumerate((0, ALIGNED - 1)):
        for i in range(2):
            for c in range(3):
                at = 6 * j + 3 * i + c
                ends[at : at + 1] = near_ends[i, j, c, row : row + 1]


def pack_kernel(held, coords, displacement, out, arrived):
    rows = 3 * held
    copies = [
        pltpu.make_async_copy(source, out.at[pl.ds(i * rows, rows)], arrived.at[i])
        for i, source in enumerate((coords, displacement))
    ]
    for copy in copies:
        copy.start()
    for copy in copies:
        copy.wait()


def frame_kernel(held, payload, near, far, out):
    end = 6 * held
    out[end : end + 12] = near[...]
    out[end + 12 : end + 24] = far[...]


def stage_kernel(held, info, own, bonds, out, left, table, arrived):
    copy = pltpu.make_async_copy(bonds, out, arrived)
    copy.start()
    base = held + EDGES
    for t in range(held):
        table[t, 0:6] = own[pl.ds(t, 6, stride=held)]

    @pl.loop(0, out.shape[0] // LEFT_GROUP)
    def _(step):
        for g in range(LEFT_GROUP):
            k = step * LEFT_GROUP + g
            here = centred(table[info[0, k] - base], info, k)
            left[k] = jnp.transpose(left_rows(here)).astype(jnp.bfloat16)

    copy.wait()


def pieces(value):
    first = value.astype(jnp.bfloat16).astype(jnp.float32)
    rest = value - first
    second = rest.astype(jnp.bfloat16).astype(jnp.float32)
    return first, second, rest - second


def middle_of(mid_x, mid_y, mid_z, points):
    row = lax.broadcasted_iota(jnp.int32, (8, points), 0)
    return jnp.where(
        row == 0, mid_x, jnp.where(row == 1, mid_y, jnp.where(row == 2, mid_z, 0.0))
    )


def centred(tile, info, k):
    mid_x = info[2, k].astype(jnp.float32) + 1.5
    mid_y = info[3, k].astype(jnp.float32) + 1.5
    return (tile - middle_of(mid_x, mid_y, MID_Z, tile.shape[-1])) * (1.0 / HORIZON)


def side_rows(here, row):
    moved = pltpu.roll(here, 5, axis=0)
    now = here + moved
    low = row < 3
    square = jnp.sum(jnp.where(low, here * here, 0.0), axis=0, keepdims=True)
    growth = jnp.sum(jnp.where(low, moved * (here + now), 0.0), axis=0, keepdims=True)
    return moved, now, square, growth


def now_rows(now, row):
    first = now.astype(jnp.bfloat16).astype(jnp.float32)
    second = now - first
    top = jnp.where(row < 3, first, jnp.where(row == 3, 1.0, 0.0))
    rows = jnp.concatenate([top, jnp.where(row < 3, second, 0.0)], axis=0)
    rows = rows.astype(jnp.bfloat16)
    return jnp.concatenate([rows, rows], axis=1)


def left_rows(here):
    row = lax.broadcasted_iota(jnp.int32, here.shape, 0)
    six = row == 6
    _, _, square, growth = side_rows(here, row)
    l1, l2, l3 = pieces(jnp.where(row < 6, -2.0 * here, jnp.where(six, square, growth)))

    def ones(value):
        return jnp.where(row < 6, value, jnp.where(six, 1.0, 0.0))

    o1, o2 = ones(l1), ones(l2)
    return jnp.concatenate([l1, l2, l3, o1, o2, o1], axis=0)


def right_rows(here):
    row = lax.broadcasted_iota(jnp.int32, here.shape, 0)
    six, seven = row == 6, row == 7
    moved, now, square, growth = side_rows(here, row)
    lowered = pltpu.roll(now, 3, axis=0)
    right_ref = jnp.where(row < 3, here, jnp.where(six, square, 0.0))
    right_gain = jnp.where(
        row < 3, moved, jnp.where(row < 6, lowered, jnp.where(six, growth, 0.0))
    )

    def stack(value, at_six, at_seven):
        p1, p2, p3 = pieces(value)
        base = jnp.where(six, at_six, jnp.where(seven, at_seven, p1))
        mixed = jnp.where(six, p1, p2)
        return jnp.concatenate([base, base, base, mixed, p2, p3], axis=0)

    return jnp.concatenate([stack(right_ref, 1.0, 0.0), stack(right_gain, 0.0, 1.0)], axis=1)


def pull_of(both, bond_mask):
    points = bond_mask.shape[-1]
    ref2, gain2 = both[:, :points], both[:, points:]
    now2 = jnp.maximum(ref2 + gain2, 1e-7)
    per_ref, per_now = lax.rsqrt(ref2), lax.rsqrt(now2)
    length_ref, length_now = ref2 * per_ref, now2 * per_now
    stretch = (gain2 * per_ref) * (1.0 / (length_now + length_ref))
    influence = jnp.maximum(1.0 - length_ref, 0.0)
    soften = jnp.clip(FINAL - stretch, 0.0, FINAL - ONSET)
    pull = ((stretch * influence) * soften) * (per_now * bond_mask.astype(jnp.float32))
    high = pull.astype(jnp.bfloat16)
    low = (pull - high.astype(jnp.float32)).astype(jnp.bfloat16)
    return high, low


def gather_pair(now_a, now_b, high, low):
    row = lax.broadcasted_iota(jnp.int32, now_a.shape, 0)
    on_b = jnp.dot(
        now_rows(now_a, row),
        jnp.concatenate([high, low], axis=0),
        preferred_element_type=jnp.float32,
    )
    on_a = lax.dot_general(
        now_rows(now_b, row),
        jnp.concatenate([high, low], axis=1),
        (((1,), (1,)), ((), ())),
        preferred_element_type=jnp.float32,
    )
    sum_a, sum_b = on_a[0:8] + on_a[8:16], on_b[0:8] + on_b[8:16]
    scale = STIFFNESS / (FINAL - ONSET)
    return scale * (sum_a - now_a * sum_a[3:4]), scale * (sum_b - now_b * sum_b[3:4])


def bond_kernel(
    held, info, below, own, above, bonds, left, force, down, up, edges,
    table, total, *rings
):
    count, points, _ = bonds.shape
    squares, pulls = rings[:RING], rings[RING:]
    span = held + EDGES
    for r, payload in enumerate((below, own, above)):
        for t in range(held):
            table[r * span + t, 0:6] = payload[pl.ds(t, 6, stride=held)]
        for i in range(EDGES):
            at = 6 * (held + i)
            table[r * span + held + i, 0:6] = payload[at : at + 6]
    total[...] = jnp.zeros_like(total)

    def measure(k, squares):
        rows = right_rows(centred(table[info[1, k]], info, k)).astype(jnp.bfloat16)
        squares[...] = jnp.dot(left[k], rows, preferred_element_type=jnp.float32)

    def visit(k, squares, pulls):
        high, low = pull_of(squares[...], bonds[k])
        pulls[0:points], pulls[points:] = high, low

    def collect(k, pulls):
        here_a = centred(table[info[0, k]], info, k)
        here_b = centred(table[info[1, k]], info, k)
        gain_a, gain_b = gather_pair(
            here_a + pltpu.roll(here_a, 5, axis=0),
            here_b + pltpu.roll(here_b, 5, axis=0),
            pulls[0:points],
            pulls[points:],
        )
        total[info[0, k]] += gain_a
        total[info[1, k]] += gain_b

    @pl.loop(0, count // GROUP)
    def _(turn):
        first = turn * GROUP
        for at in range(GROUP + 2 * LAG):
            if at < GROUP:
                measure(first + at, squares[at % RING])
            if 0 <= at - LAG < GROUP:
                visit(first + at - LAG, squares[(at - LAG) % RING], pulls[(at - LAG) % RING])
            if 0 <= at - 2 * LAG < GROUP:
                collect(first + at - 2 * LAG, pulls[(at - 2 * LAG) % RING])

    for r, out in enumerate((down, force, up)):
        for t in range(held):
            out[pl.ds(t, 3, stride=held)] = total[r * span + t, 0:3]
    for r, out, at in ((0, down, 3 * held), (1, edges, 0), (2, up, 3 * held)):
        for i in range(EDGES):
            out[at + 3 * i : at + 3 * i + 3] = total[r * span + held + i, 0:3]
    for out in (down, up):
        end = 3 * span
        if end < out.shape[0]:
            out[end:] = jnp.zeros((out.shape[0] - end, out.shape[1]), jnp.float32)


def merge_kernel(held, force, from_above, from_below, near, far, out):
    rows = 3 * held
    out[...] = force[...] + (from_above[0:rows] + from_below[0:rows])
    out[pl.ds(0, 3, stride=held)] += near[0:3] + far[0:3]
    out[pl.ds(held - 1, 3, stride=held)] += near[3:6] + far[3:6]


def limit(mebibytes):
    return pltpu.CompilerParams(vmem_limit_bytes=mebibytes * 1024 * 1024)


def stage_call(held, intact):
    count, points, _ = intact.shape
    return pl.pallas_call(
        functools.partial(stage_kernel, held),
        out_shape=(
            jax.ShapeDtypeStruct(intact.shape, intact.dtype),
            jax.ShapeDtypeStruct((count, points, 48), jnp.bfloat16),
        ),
        in_specs=[SMEM, VMEM, HBM],
        out_specs=(VMEM, VMEM),
        scratch_shapes=[
            pltpu.VMEM((held, 8, points), jnp.float32),
            pltpu.SemaphoreType.DMA,
        ],
        compiler_params=limit(2),
        cost_estimate=pl.CostEstimate(
            flops=0, bytes_accessed=4 * intact.size, transcendentals=0
        ),
        name="stage_bonds",
    )


def bond_call(held, count, points):
    span = held + EDGES
    f32 = jnp.float32
    sent = jax.ShapeDtypeStruct((padded_rows(3 * span), points), f32)
    return pl.pallas_call(
        functools.partial(bond_kernel, held),
        out_shape=(
            jax.ShapeDtypeStruct((3 * held, points), f32),
            sent,
            sent,
            jax.ShapeDtypeStruct((3 * EDGES, points), f32),
        ),
        in_specs=[SMEM] + [VMEM] * 5,
        out_specs=(VMEM,) * 4,
        scratch_shapes=[pltpu.VMEM((3 * span, 8, points), f32)] * 2
        + [pltpu.VMEM((points, 2 * points), f32)] * RING
        + [pltpu.VMEM((2 * points, points), jnp.bfloat16)] * RING,
        compiler_params=limit(8),
        name="bond_forces",
    )


def swapped(value, axis, phase):
    pairs = []
    for i in range(phase, lax.axis_size(axis) - 1, 2):
        pairs += [(i, i + 1), (i + 1, i)]
    return lax.ppermute(value, axis, pairs)


def on_device(coords, displacement, pairs, intact):
    held, _, points = coords.shape
    span = held + EDGES
    strip_tiles = held * lax.axis_size("tile")
    f32 = jnp.float32

    packed = jax.ShapeDtypeStruct((padded_rows(6 * span), points), f32)
    places, shifts = jnp.transpose(coords, (1, 0, 2)), jnp.transpose(displacement, (1, 0, 2))
    ends = pl.pallas_call(
        ends_kernel,
        out_shape=jax.ShapeDtypeStruct((12, points), f32),
        in_specs=[HBM] * 2,
        out_specs=VMEM,
        scratch_shapes=[
            pltpu.VMEM((2, 2, 3, ALIGNED, points), f32),
            pltpu.SemaphoreType.DMA((4,)),
        ],
        compiler_params=limit(1),
        name="end_tiles",
    )(in_hbm(places), in_hbm(shifts))
    inside = pl.pallas_call(
        functools.partial(pack_kernel, held),
        out_shape=packed,
        in_specs=[HBM] * 2,
        out_specs=VMEM,
        scratch_shapes=[pltpu.SemaphoreType.DMA((2,))],
        compiler_params=limit(1),
        cost_estimate=pl.CostEstimate(flops=0, bytes_accessed=4 << 20, transcendentals=0),
        name="pack_payload",
    )(in_hbm(places.reshape(-1, points)), in_hbm(shifts.reshape(-1, points)))
    near = swapped(ends, "tile", 0)
    far = swapped(ends, "tile", 1)

    own = pl.pallas_call(
        functools.partial(frame_kernel, held),
        out_shape=packed,
        in_specs=[VMEM] * 3,
        out_specs=VMEM,
        input_output_aliases={0: 0},
        compiler_params=limit(1),
        name="frame_payload",
    )(inside, near, far)
    below = shifted(own, "strip", 1)
    above = shifted(own, "strip", -1)
    own, pairs = lax.optimization_barrier((own, pairs))
    tile_index = lax.axis_index("tile")
    strip_of, place = pairs // strip_tiles, pairs % strip_tiles
    row = strip_of - lax.axis_index("strip") + 1
    local = place - tile_index * held
    odd = tile_index % 2
    column = jnp.where(
        local < 0, held + 3 - 2 * odd, jnp.where(local >= held, held + 2 * odd, local)
    )
    slots = row * span + column
    info = jnp.stack(
        [
            slots[:, 0],
            slots[:, 1],
            2 * (strip_of[:, 0] + strip_of[:, 1]),
            2 * (place[:, 0] + place[:, 1]),
        ]
    )

    bonds, left = stage_call(held, intact)(info, own, in_hbm(intact))
    force, down, up, edges = bond_call(held, intact.shape[0], points)(
        info, below, own, above, bonds, left
    )
    from_above = shifted(down, "strip", -1)
    from_below = shifted(up, "strip", 1)
    tail = slice(3 * held, 3 * span)
    edge = edges + (from_above[tail] + from_below[tail])
    near_force = swapped(edge[0:6], "tile", 0)
    far_force = swapped(edge[6:12], "tile", 1)
    merged = pl.pallas_call(
        functools.partial(merge_kernel, held),
        out_shape=jax.ShapeDtypeStruct((3 * held, points), f32),
        in_specs=[VMEM] * 5,
        out_specs=VMEM,
        compiler_params=limit(1),
        name="merge_forces",
    )(force, from_above, from_below, near_force, far_force)
    return jnp.transpose(merged.reshape(3, held, points), (1, 0, 2))


def solution(mesh):
    placed = P(("strip", "tile"), None, None)
    return jax.shard_map(
        on_device,
        mesh=mesh,
        in_specs=(placed, placed, P(("strip", "tile"), None), placed),
        out_specs=placed,
        check_vma=False,
    )
```

```python
import functools

import jax
import jax.numpy as jnp
from jax import lax
from jax.experimental import pallas as pl
from jax.experimental.pallas import tpu as pltpu
from jax.sharding import PartitionSpec as P

HORIZON = 3.0
STIFFNESS = 2.0
ONSET = 0.02
FINAL = 0.05

GROUP = 64
LAG = 3
RING = 6
LEFT_GROUP = 8
MID_Z = 3.5
EDGES = 4
ALIGNED = 8
VMEM = pl.BlockSpec(memory_space=pltpu.VMEM)
HBM = pl.BlockSpec(memory_space=pltpu.HBM)
SMEM = pl.BlockSpec(memory_space=pltpu.SMEM)


def shifted(value, axis, step):
    count = lax.axis_size(axis)
    first, last = max(0, -step), min(count, count - step)
    return lax.ppermute(value, axis, [(i, i + step) for i in range(first, last)])


def in_hbm(value):
    return pltpu.with_memory_space_constraint(value, pltpu.HBM)


def padded_rows(rows):
    return (rows + 7) // 8 * 8


def ends_kernel(coords, displacement, ends, near_ends, arrived):
    held = coords.shape[1]
    copies = []
    for i, source in enumerate((coords, displacement)):
        for j, start in enumerate((0, held - ALIGNED)):
            copies.append(
                pltpu.make_async_copy(
                    source.at[:, pl.ds(start, ALIGNED), :],
                    near_ends.at[i, j],
                    arrived.at[2 * i + j],
                )
            )
    for copy in copies:
        copy.start()
    for copy in copies:
        copy.wait()
    for j, row in enumerate((0, ALIGNED - 1)):
        for i in range(2):
            for c in range(3):
                at = 6 * j + 3 * i + c
                ends[at : at + 1] = near_ends[i, j, c, row : row + 1]


def pack_kernel(held, coords, displacement, out, arrived):
    rows = 3 * held
    copies = [
        pltpu.make_async_copy(source, out.at[pl.ds(i * rows, rows)], arrived.at[i])
        for i, source in enumerate((coords, displacement))
    ]
    for copy in copies:
        copy.start()
    for copy in copies:
        copy.wait()


def frame_kernel(held, payload, near, far, out):
    end = 6 * held
    out[end : end + 12] = near[...]
    out[end + 12 : end + 24] = far[...]


def stage_kernel(held, info, own, bonds, out, left, table, arrived):
    copy = pltpu.make_async_copy(bonds, out, arrived)
    copy.start()
    base = held + EDGES
    for t in range(held):
        table[t, 0:6] = own[pl.ds(t, 6, stride=held)]

    @pl.loop(0, out.shape[0] // LEFT_GROUP)
    def _(step):
        for g in range(LEFT_GROUP):
            k = step * LEFT_GROUP + g
            here = centred(table[info[0, k] - base], info, k)
            left[k] = jnp.transpose(left_rows(here)).astype(jnp.bfloat16)

    copy.wait()


def pieces(value):
    first = value.astype(jnp.bfloat16).astype(jnp.float32)
    rest = value - first
    second = rest.astype(jnp.bfloat16).astype(jnp.float32)
    return first, second, rest - second


def middle_of(mid_x, mid_y, mid_z, points):
    row = lax.broadcasted_iota(jnp.int32, (8, points), 0)
    return jnp.where(
        row == 0, mid_x, jnp.where(row == 1, mid_y, jnp.where(row == 2, mid_z, 0.0))
    )


def centred(tile, info, k):
    mid_x = info[2, k].astype(jnp.float32) + 1.5
    mid_y = info[3, k].astype(jnp.float32) + 1.5
    return (tile - middle_of(mid_x, mid_y, MID_Z, tile.shape[-1])) * (1.0 / HORIZON)


def side_rows(here, row):
    moved = pltpu.roll(here, 5, axis=0)
    now = here + moved
    low = row < 3
    square = jnp.sum(jnp.where(low, here * here, 0.0), axis=0, keepdims=True)
    growth = jnp.sum(jnp.where(low, moved * (here + now), 0.0), axis=0, keepdims=True)
    return moved, now, square, growth


def now_rows(now, row):
    first = now.astype(jnp.bfloat16).astype(jnp.float32)
    second = now - first
    top = jnp.where(row < 3, first, jnp.where(row == 3, 1.0, 0.0))
    rows = jnp.concatenate([top, jnp.where(row < 3, second, 0.0)], axis=0)
    rows = rows.astype(jnp.bfloat16)
    return jnp.concatenate([rows, rows], axis=1)


def left_rows(here):
    row = lax.broadcasted_iota(jnp.int32, here.shape, 0)
    six = row == 6
    _, _, square, growth = side_rows(here, row)
    l1, l2, l3 = pieces(jnp.where(row < 6, -2.0 * here, jnp.where(six, square, growth)))

    def ones(value):
        return jnp.where(row < 6, value, jnp.where(six, 1.0, 0.0))

    o1, o2 = ones(l1), ones(l2)
    return jnp.concatenate([l1, l2, l3, o1, o2, o1], axis=0)


def right_rows(here):
    row = lax.broadcasted_iota(jnp.int32, here.shape, 0)
    six, seven = row == 6, row == 7
    moved, now, square, growth = side_rows(here, row)
    lowered = pltpu.roll(now, 3, axis=0)
    right_ref = jnp.where(row < 3, here, jnp.where(six, square, 0.0))
    right_gain = jnp.where(
        row < 3, moved, jnp.where(row < 6, lowered, jnp.where(six, growth, 0.0))
    )

    def stack(value, at_six, at_seven):
        p1, p2, p3 = pieces(value)
        base = jnp.where(six, at_six, jnp.where(seven, at_seven, p1))
        mixed = jnp.where(six, p1, p2)
        return jnp.concatenate([base, base, base, mixed, p2, p3], axis=0)

    return jnp.concatenate([stack(right_ref, 1.0, 0.0), stack(right_gain, 0.0, 1.0)], axis=1)


def pull_of(both, bond_mask):
    points = bond_mask.shape[-1]
    ref2, gain2 = both[:, :points], both[:, points:]
    now2 = jnp.maximum(ref2 + gain2, 1e-7)
    per_ref, per_now = lax.rsqrt(ref2), lax.rsqrt(now2)
    length_ref, length_now = ref2 * per_ref, now2 * per_now
    stretch = (gain2 * per_ref) * (1.0 / (length_now + length_ref))
    influence = jnp.maximum(1.0 - length_ref, 0.0)
    soften = jnp.clip(FINAL - stretch, 0.0, FINAL - ONSET)
    pull = ((stretch * influence) * soften) * (per_now * bond_mask.astype(jnp.float32))
    high = pull.astype(jnp.bfloat16)
    low = (pull - high.astype(jnp.float32)).astype(jnp.bfloat16)
    return high, low


def gather_pair(now_a, now_b, high, low):
    row = lax.broadcasted_iota(jnp.int32, now_a.shape, 0)
    on_b = jnp.dot(
        now_rows(now_a, row),
        jnp.concatenate([high, low], axis=0),
        preferred_element_type=jnp.float32,
    )
    on_a = lax.dot_general(
        now_rows(now_b, row),
        jnp.concatenate([high, low], axis=1),
        (((1,), (1,)), ((), ())),
        preferred_element_type=jnp.float32,
    )
    sum_a, sum_b = on_a[0:8] + on_a[8:16], on_b[0:8] + on_b[8:16]
    scale = STIFFNESS / (FINAL - ONSET)
    return scale * (sum_a - now_a * sum_a[3:4]), scale * (sum_b - now_b * sum_b[3:4])


def bond_kernel(
    held, info, below, own, above, bonds, left, force, down, up, edges,
    table, total, *rings
):
    count, points, _ = bonds.shape
    squares, pulls = rings[:RING], rings[RING:]
    span = held + EDGES
    for r, payload in enumerate((below, own, above)):
        for t in range(held):
            table[r * span + t, 0:6] = payload[pl.ds(t, 6, stride=held)]
        for i in range(EDGES):
            at = 6 * (held + i)
            table[r * span + held + i, 0:6] = payload[at : at + 6]
    total[...] = jnp.zeros_like(total)

    def measure(k, squares):
        rows = right_rows(centred(table[info[1, k]], info, k)).astype(jnp.bfloat16)
        squares[...] = jnp.dot(left[k], rows, preferred_element_type=jnp.float32)

    def visit(k, squares, pulls):
        high, low = pull_of(squares[...], bonds[k])
        pulls[0:points], pulls[points:] = high, low

    def collect(k, pulls):
        here_a = centred(table[info[0, k]], info, k)
        here_b = centred(table[info[1, k]], info, k)
        gain_a, gain_b = gather_pair(
            here_a + pltpu.roll(here_a, 5, axis=0),
            here_b + pltpu.roll(here_b, 5, axis=0),
            pulls[0:points],
            pulls[points:],
        )
        total[info[0, k]] += gain_a
        total[info[1, k]] += gain_b

    @pl.loop(0, count // GROUP)
    def _(turn):
        first = turn * GROUP
        for at in range(GROUP + 2 * LAG):
            if at < GROUP:
                measure(first + at, squares[at % RING])
            if 0 <= at - LAG < GROUP:
                visit(first + at - LAG, squares[(at - LAG) % RING], pulls[(at - LAG) % RING])
            if 0 <= at - 2 * LAG < GROUP:
                collect(first + at - 2 * LAG, pulls[(at - 2 * LAG) % RING])

    for r, out in enumerate((down, force, up)):
        for t in range(held):
            out[pl.ds(t, 3, stride=held)] = total[r * span + t, 0:3]
    for r, out, at in ((0, down, 3 * held), (1, edges, 0), (2, up, 3 * held)):
        for i in range(EDGES):
            out[at + 3 * i : at + 3 * i + 3] = total[r * span + held + i, 0:3]
    for out in (down, up):
        end = 3 * span
        if end < out.shape[0]:
            out[end:] = jnp.zeros((out.shape[0] - end, out.shape[1]), jnp.float32)


def merge_kernel(held, force, from_below, from_above, near, far, out):
    rows = 3 * held
    out[...] = force[...] + (from_below[0:rows] + from_above[0:rows])
    out[pl.ds(0, 3, stride=held)] += near[0:3] + far[0:3]
    out[pl.ds(held - 1, 3, stride=held)] += near[3:6] + far[3:6]


def limit(mebibytes):
    return pltpu.CompilerParams(vmem_limit_bytes=mebibytes * 1024 * 1024)


def stage_call(held, intact):
    count, points, _ = intact.shape
    return pl.pallas_call(
        functools.partial(stage_kernel, held),
        out_shape=(
            jax.ShapeDtypeStruct(intact.shape, intact.dtype),
            jax.ShapeDtypeStruct((count, points, 48), jnp.bfloat16),
        ),
        in_specs=[SMEM, VMEM, HBM],
        out_specs=(VMEM, VMEM),
        scratch_shapes=[
            pltpu.VMEM((held, 8, points), jnp.float32),
            pltpu.SemaphoreType.DMA,
        ],
        compiler_params=limit(2),
        cost_estimate=pl.CostEstimate(
            flops=0, bytes_accessed=4 * intact.size, transcendentals=0
        ),
        name="stage_bonds",
    )


def bond_call(held, count, points):
    span = held + EDGES
    f32 = jnp.float32
    sent = jax.ShapeDtypeStruct((padded_rows(3 * span), points), f32)
    return pl.pallas_call(
        functools.partial(bond_kernel, held),
        out_shape=(
            jax.ShapeDtypeStruct((3 * held, points), f32),
            sent,
            sent,
            jax.ShapeDtypeStruct((3 * EDGES, points), f32),
        ),
        in_specs=[SMEM] + [VMEM] * 5,
        out_specs=(VMEM,) * 4,
        scratch_shapes=[pltpu.VMEM((3 * span, 8, points), f32)] * 2
        + [pltpu.VMEM((points, 2 * points), f32)] * RING
        + [pltpu.VMEM((2 * points, points), jnp.bfloat16)] * RING,
        compiler_params=limit(8),
        name="bond_forces",
    )


def swapped(value, axis, phase):
    pairs = []
    for i in range(phase, lax.axis_size(axis) - 1, 2):
        pairs += [(i, i + 1), (i + 1, i)]
    return lax.ppermute(value, axis, pairs)


def on_device(coords, displacement, pairs, intact):
    held, _, points = coords.shape
    span = held + EDGES
    strip_tiles = held * lax.axis_size("tile")
    f32 = jnp.float32

    packed = jax.ShapeDtypeStruct((padded_rows(6 * span), points), f32)
    places, shifts = jnp.transpose(coords, (1, 0, 2)), jnp.transpose(displacement, (1, 0, 2))
    ends = pl.pallas_call(
        ends_kernel,
        out_shape=jax.ShapeDtypeStruct((12, points), f32),
        in_specs=[HBM] * 2,
        out_specs=VMEM,
        scratch_shapes=[
            pltpu.VMEM((2, 2, 3, ALIGNED, points), f32),
            pltpu.SemaphoreType.DMA((4,)),
        ],
        compiler_params=limit(1),
        name="end_tiles",
    )(in_hbm(places), in_hbm(shifts))
    inside = pl.pallas_call(
        functools.partial(pack_kernel, held),
        out_shape=packed,
        in_specs=[HBM] * 2,
        out_specs=VMEM,
        scratch_shapes=[pltpu.SemaphoreType.DMA((2,))],
        compiler_params=limit(1),
        cost_estimate=pl.CostEstimate(flops=0, bytes_accessed=4 << 20, transcendentals=0),
        name="pack_payload",
    )(in_hbm(places.reshape(-1, points)), in_hbm(shifts.reshape(-1, points)))
    near = swapped(ends, "tile", 0)
    far = swapped(ends, "tile", 1)

    own = pl.pallas_call(
        functools.partial(frame_kernel, held),
        out_shape=packed,
        in_specs=[VMEM] * 3,
        out_specs=VMEM,
        input_output_aliases={0: 0},
        compiler_params=limit(1),
        name="frame_payload",
    )(inside, near, far)
    below = shifted(own, "strip", 1)
    above = shifted(own, "strip", -1)
    own, pairs = lax.optimization_barrier((own, pairs))
    tile_index = lax.axis_index("tile")
    strip_of, place = pairs // strip_tiles, pairs % strip_tiles
    row = strip_of - lax.axis_index("strip") + 1
    local = place - tile_index * held
    odd = tile_index % 2
    column = jnp.where(
        local < 0, held + 3 - 2 * odd, jnp.where(local >= held, held + 2 * odd, local)
    )
    slots = row * span + column
    info = jnp.stack(
        [
            slots[:, 0],
            slots[:, 1],
            2 * (strip_of[:, 0] + strip_of[:, 1]),
            2 * (place[:, 0] + place[:, 1]),
        ]
    )

    bonds, left = stage_call(held, intact)(info, own, in_hbm(intact))
    force, down, up, edges = bond_call(held, intact.shape[0], points)(
        info, below, own, above, bonds, left
    )
    from_below = shifted(up, "strip", 1)
    from_above = shifted(down, "strip", -1)
    tail = slice(3 * held, 3 * span)
    edge = edges + (from_below[tail] + from_above[tail])
    near_force = swapped(edge[0:6], "tile", 0)
    far_force = swapped(edge[6:12], "tile", 1)
    merged = pl.pallas_call(
        functools.partial(merge_kernel, held),
        out_shape=jax.ShapeDtypeStruct((3 * held, points), f32),
        in_specs=[VMEM] * 5,
        out_specs=VMEM,
        compiler_params=limit(1),
        name="merge_forces",
    )(force, from_below, from_above, near_force, far_force)
    return jnp.transpose(merged.reshape(3, held, points), (1, 0, 2))


def solution(mesh):
    placed = P(("strip", "tile"), None, None)
    return jax.shard_map(
        on_device,
        mesh=mesh,
        in_specs=(placed, placed, P(("strip", "tile"), None), placed),
        out_specs=placed,
        check_vma=False,
    )
```

```python
import functools

import jax
import jax.numpy as jnp
from jax import lax
from jax.experimental import pallas as pl
from jax.experimental.pallas import tpu as pltpu
from jax.sharding import PartitionSpec as P

HORIZON = 3.0
STIFFNESS = 2.0
ONSET = 0.02
FINAL = 0.05

GROUP = 64
LAG = 3
RING = 6
LEFT_GROUP = 8
MID_Z = 3.5
EDGES = 4
ALIGNED = 8
VMEM = pl.BlockSpec(memory_space=pltpu.VMEM)
HBM = pl.BlockSpec(memory_space=pltpu.HBM)
SMEM = pl.BlockSpec(memory_space=pltpu.SMEM)


def shifted(value, axis, step):
    count = lax.axis_size(axis)
    first, last = max(0, -step), min(count, count - step)
    return lax.ppermute(value, axis, [(i, i + step) for i in range(first, last)])


def in_hbm(value):
    return pltpu.with_memory_space_constraint(value, pltpu.HBM)


def padded_rows(rows):
    return (rows + 7) // 8 * 8


def ends_kernel(coords, displacement, ends, near_ends, arrived):
    held = coords.shape[1]
    copies = []
    for i, source in enumerate((coords, displacement)):
        for j, start in enumerate((0, held - ALIGNED)):
            copies.append(
                pltpu.make_async_copy(
                    source.at[:, pl.ds(start, ALIGNED), :],
                    near_ends.at[i, j],
                    arrived.at[2 * i + j],
                )
            )
    for copy in copies:
        copy.start()
    for copy in copies:
        copy.wait()
    for j, row in enumerate((0, ALIGNED - 1)):
        for i in range(2):
            for c in range(3):
                at = 6 * j + 3 * i + c
                ends[at : at + 1] = near_ends[i, j, c, row : row + 1]


def pack_kernel(held, coords, displacement, out, arrived):
    rows = 3 * held
    copies = [
        pltpu.make_async_copy(source, out.at[pl.ds(i * rows, rows)], arrived.at[i])
        for i, source in enumerate((coords, displacement))
    ]
    for copy in copies:
        copy.start()
    for copy in copies:
        copy.wait()


def frame_kernel(held, payload, near, far, out):
    end = 6 * held
    out[end : end + 12] = near[...]
    out[end + 12 : end + 24] = far[...]


def stage_kernel(held, info, own, bonds, out, left, table, arrived):
    copy = pltpu.make_async_copy(bonds, out, arrived)
    copy.start()
    base = held + EDGES
    for t in range(held):
        table[t, 0:6] = own[pl.ds(t, 6, stride=held)]

    @pl.loop(0, out.shape[0] // LEFT_GROUP)
    def _(step):
        for g in range(LEFT_GROUP):
            k = step * LEFT_GROUP + g
            here = centred(table[info[0, k] - base], info, k)
            left[k] = jnp.transpose(left_rows(here)).astype(jnp.bfloat16)

    copy.wait()


def pieces(value):
    first = value.astype(jnp.bfloat16).astype(jnp.float32)
    rest = value - first
    second = rest.astype(jnp.bfloat16).astype(jnp.float32)
    return first, second, rest - second


def middle_of(mid_x, mid_y, mid_z, points):
    row = lax.broadcasted_iota(jnp.int32, (8, points), 0)
    return jnp.where(
        row == 0, mid_x, jnp.where(row == 1, mid_y, jnp.where(row == 2, mid_z, 0.0))
    )


def centred(tile, info, k):
    mid_x = info[2, k].astype(jnp.float32) + 1.5
    mid_y = info[3, k].astype(jnp.float32) + 1.5
    return (tile - middle_of(mid_x, mid_y, MID_Z, tile.shape[-1])) * (1.0 / HORIZON)


def side_rows(here, row):
    moved = pltpu.roll(here, 5, axis=0)
    now = here + moved
    low = row < 3
    square = jnp.sum(jnp.where(low, here * here, 0.0), axis=0, keepdims=True)
    growth = jnp.sum(jnp.where(low, moved * (here + now), 0.0), axis=0, keepdims=True)
    return moved, now, square, growth


def now_rows(now, row):
    first = now.astype(jnp.bfloat16).astype(jnp.float32)
    second = now - first
    top = jnp.where(row < 3, first, jnp.where(row == 3, 1.0, 0.0))
    rows = jnp.concatenate([top, jnp.where(row < 3, second, 0.0)], axis=0)
    rows = rows.astype(jnp.bfloat16)
    return jnp.concatenate([rows, rows], axis=1)


def left_rows(here):
    row = lax.broadcasted_iota(jnp.int32, here.shape, 0)
    six = row == 6
    _, _, square, growth = side_rows(here, row)
    l1, l2, l3 = pieces(jnp.where(row < 6, -2.0 * here, jnp.where(six, square, growth)))

    def ones(value):
        return jnp.where(row < 6, value, jnp.where(six, 1.0, 0.0))

    o1, o2 = ones(l1), ones(l2)
    return jnp.concatenate([l1, l2, l3, o1, o2, o1], axis=0)


def right_rows(here):
    row = lax.broadcasted_iota(jnp.int32, here.shape, 0)
    six, seven = row == 6, row == 7
    moved, now, square, growth = side_rows(here, row)
    lowered = pltpu.roll(now, 3, axis=0)
    right_ref = jnp.where(row < 3, here, jnp.where(six, square, 0.0))
    right_gain = jnp.where(
        row < 3, moved, jnp.where(row < 6, lowered, jnp.where(six, growth, 0.0))
    )

    def stack(value, at_six, at_seven):
        p1, p2, p3 = pieces(value)
        base = jnp.where(six, at_six, jnp.where(seven, at_seven, p1))
        mixed = jnp.where(six, p1, p2)
        return jnp.concatenate([base, base, base, mixed, p2, p3], axis=0)

    return jnp.concatenate([stack(right_ref, 1.0, 0.0), stack(right_gain, 0.0, 1.0)], axis=1)


def pull_of(both, bond_mask):
    points = bond_mask.shape[-1]
    ref2, gain2 = both[:, :points], both[:, points:]
    now2 = jnp.maximum(ref2 + gain2, 1e-7)
    per_ref, per_now = lax.rsqrt(ref2), lax.rsqrt(now2)
    length_ref, length_now = ref2 * per_ref, now2 * per_now
    stretch = (gain2 * per_ref) * (1.0 / (length_now + length_ref))
    influence = jnp.maximum(1.0 - length_ref, 0.0)
    soften = jnp.clip(FINAL - stretch, 0.0, FINAL - ONSET)
    pull = ((stretch * influence) * soften) * (per_now * bond_mask.astype(jnp.float32))
    high = pull.astype(jnp.bfloat16)
    low = (pull - high.astype(jnp.float32)).astype(jnp.bfloat16)
    return high, low


def gather_pair(now_a, now_b, high, low):
    row = lax.broadcasted_iota(jnp.int32, now_a.shape, 0)
    on_b = jnp.dot(
        now_rows(now_a, row),
        jnp.concatenate([high, low], axis=0),
        preferred_element_type=jnp.float32,
    )
    on_a = lax.dot_general(
        now_rows(now_b, row),
        jnp.concatenate([high, low], axis=1),
        (((1,), (1,)), ((), ())),
        preferred_element_type=jnp.float32,
    )
    sum_a, sum_b = on_a[0:8] + on_a[8:16], on_b[0:8] + on_b[8:16]
    scale = STIFFNESS / (FINAL - ONSET)
    return scale * (sum_a - now_a * sum_a[3:4]), scale * (sum_b - now_b * sum_b[3:4])


def bond_kernel(
    held, info, below, own, above, bonds, left, force, down, up, edges,
    table, total, *rings
):
    count, points, _ = bonds.shape
    squares, pulls = rings[:RING], rings[RING:]
    span = held + EDGES
    for r, payload in enumerate((below, own, above)):
        for t in range(held):
            table[r * span + t, 0:6] = payload[pl.ds(t, 6, stride=held)]
        for i in range(EDGES):
            at = 6 * (held + i)
            table[r * span + held + i, 0:6] = payload[at : at + 6]
    total[...] = jnp.zeros_like(total)

    def measure(k, squares):
        rows = right_rows(centred(table[info[1, k]], info, k)).astype(jnp.bfloat16)
        squares[...] = jnp.dot(left[k], rows, preferred_element_type=jnp.float32)

    def visit(k, squares, pulls):
        high, low = pull_of(squares[...], bonds[k])
        pulls[0:points], pulls[points:] = high, low

    def collect(k, pulls):
        here_a = centred(table[info[0, k]], info, k)
        here_b = centred(table[info[1, k]], info, k)
        gain_a, gain_b = gather_pair(
            here_a + pltpu.roll(here_a, 5, axis=0),
            here_b + pltpu.roll(here_b, 5, axis=0),
            pulls[0:points],
            pulls[points:],
        )
        total[info[0, k]] += gain_a
        total[info[1, k]] += gain_b

    @pl.loop(0, count // GROUP)
    def _(turn):
        first = turn * GROUP
        for at in range(GROUP + 2 * LAG):
            if at < GROUP:
                measure(first + at, squares[at % RING])
            if 0 <= at - LAG < GROUP:
                visit(first + at - LAG, squares[(at - LAG) % RING], pulls[(at - LAG) % RING])
            if 0 <= at - 2 * LAG < GROUP:
                collect(first + at - 2 * LAG, pulls[(at - 2 * LAG) % RING])

    for r, out in enumerate((down, force, up)):
        for t in range(held):
            out[pl.ds(t, 3, stride=held)] = total[r * span + t, 0:3]
    for r, out, at in ((0, down, 3 * held), (1, edges, 0), (2, up, 3 * held)):
        for i in range(EDGES):
            out[at + 3 * i : at + 3 * i + 3] = total[r * span + held + i, 0:3]
    for out in (down, up):
        end = 3 * span
        if end < out.shape[0]:
            out[end:] = jnp.zeros((out.shape[0] - end, out.shape[1]), jnp.float32)


def merge_kernel(held, force, from_above, from_below, out, blocks):
    rows = 3 * held
    out[...] = force[...] + (from_above[0:rows] + from_below[0:rows])
    for j, start in enumerate((0, held - ALIGNED)):
        for c in range(3):
            blocks[j, c] = out[c * held + start : c * held + start + ALIGNED]


def finish_kernel(held, merged, blocks, near, far, out, ready, sent):
    ready[...] = blocks[...]
    for j, row in enumerate((0, ALIGNED - 1)):
        for c in range(3):
            at = 3 * j + c
            ready[j, c, row : row + 1] += near[at : at + 1] + far[at : at + 1]
    copies = []
    for j, start in enumerate((0, held - ALIGNED)):
        part = out.at[:, pl.ds(start, ALIGNED), :]
        copies.append(pltpu.make_async_copy(ready.at[j], part, sent.at[j]))
    for copy in copies:
        copy.start()
    for copy in copies:
        copy.wait()


def limit(mebibytes):
    return pltpu.CompilerParams(vmem_limit_bytes=mebibytes * 1024 * 1024)


def stage_call(held, intact):
    count, points, _ = intact.shape
    return pl.pallas_call(
        functools.partial(stage_kernel, held),
        out_shape=(
            jax.ShapeDtypeStruct(intact.shape, intact.dtype),
            jax.ShapeDtypeStruct((count, points, 48), jnp.bfloat16),
        ),
        in_specs=[SMEM, VMEM, HBM],
        out_specs=(VMEM, VMEM),
        scratch_shapes=[
            pltpu.VMEM((held, 8, points), jnp.float32),
            pltpu.SemaphoreType.DMA,
        ],
        compiler_params=limit(2),
        cost_estimate=pl.CostEstimate(
            flops=0, bytes_accessed=4 * intact.size, transcendentals=0
        ),
        name="stage_bonds",
    )


def bond_call(held, count, points):
    span = held + EDGES
    f32 = jnp.float32
    sent = jax.ShapeDtypeStruct((padded_rows(3 * span), points), f32)
    return pl.pallas_call(
        functools.partial(bond_kernel, held),
        out_shape=(
            jax.ShapeDtypeStruct((3 * held, points), f32),
            sent,
            sent,
            jax.ShapeDtypeStruct((3 * EDGES, points), f32),
        ),
        in_specs=[SMEM] + [VMEM] * 5,
        out_specs=(VMEM,) * 4,
        scratch_shapes=[pltpu.VMEM((3 * span, 8, points), f32)] * 2
        + [pltpu.VMEM((points, 2 * points), f32)] * RING
        + [pltpu.VMEM((2 * points, points), jnp.bfloat16)] * RING,
        compiler_params=limit(8),
        name="bond_forces",
    )


def swapped(value, axis, phase):
    pairs = []
    for i in range(phase, lax.axis_size(axis) - 1, 2):
        pairs += [(i, i + 1), (i + 1, i)]
    return lax.ppermute(value, axis, pairs)


def on_device(coords, displacement, pairs, intact):
    held, _, points = coords.shape
    span = held + EDGES
    strip_tiles = held * lax.axis_size("tile")
    f32 = jnp.float32

    packed = jax.ShapeDtypeStruct((padded_rows(6 * span), points), f32)
    places, shifts = jnp.transpose(coords, (1, 0, 2)), jnp.transpose(displacement, (1, 0, 2))
    ends = pl.pallas_call(
        ends_kernel,
        out_shape=jax.ShapeDtypeStruct((12, points), f32),
        in_specs=[HBM] * 2,
        out_specs=VMEM,
        scratch_shapes=[
            pltpu.VMEM((2, 2, 3, ALIGNED, points), f32),
            pltpu.SemaphoreType.DMA((4,)),
        ],
        compiler_params=limit(1),
        name="end_tiles",
    )(in_hbm(places), in_hbm(shifts))
    inside = pl.pallas_call(
        functools.partial(pack_kernel, held),
        out_shape=packed,
        in_specs=[HBM] * 2,
        out_specs=VMEM,
        scratch_shapes=[pltpu.SemaphoreType.DMA((2,))],
        compiler_params=limit(1),
        cost_estimate=pl.CostEstimate(flops=0, bytes_accessed=4 << 20, transcendentals=0),
        name="pack_payload",
    )(in_hbm(places.reshape(-1, points)), in_hbm(shifts.reshape(-1, points)))
    near = swapped(ends, "tile", 0)
    far = swapped(ends, "tile", 1)

    own = pl.pallas_call(
        functools.partial(frame_kernel, held),
        out_shape=packed,
        in_specs=[VMEM] * 3,
        out_specs=VMEM,
        input_output_aliases={0: 0},
        compiler_params=limit(1),
        name="frame_payload",
    )(inside, near, far)
    below = shifted(own, "strip", 1)
    above = shifted(own, "strip", -1)
    own, pairs = lax.optimization_barrier((own, pairs))
    tile_index = lax.axis_index("tile")
    strip_of, place = pairs // strip_tiles, pairs % strip_tiles
    row = strip_of - lax.axis_index("strip") + 1
    local = place - tile_index * held
    odd = tile_index % 2
    column = jnp.where(
        local < 0, held + 3 - 2 * odd, jnp.where(local >= held, held + 2 * odd, local)
    )
    slots = row * span + column
    info = jnp.stack(
        [
            slots[:, 0],
            slots[:, 1],
            2 * (strip_of[:, 0] + strip_of[:, 1]),
            2 * (place[:, 0] + place[:, 1]),
        ]
    )

    bonds, left = stage_call(held, intact)(info, own, in_hbm(intact))
    force, down, up, edges = bond_call(held, intact.shape[0], points)(
        info, below, own, above, bonds, left
    )
    from_above = shifted(down, "strip", -1)
    from_below = shifted(up, "strip", 1)
    tail = slice(3 * held, 3 * span)
    edge = edges + (from_above[tail] + from_below[tail])
    near_force = swapped(edge[0:6], "tile", 0)
    far_force = swapped(edge[6:12], "tile", 1)
    merged, blocks = pl.pallas_call(
        functools.partial(merge_kernel, held),
        out_shape=(
            jax.ShapeDtypeStruct((3 * held, points), f32),
            jax.ShapeDtypeStruct((2, 3, ALIGNED, points), f32),
        ),
        in_specs=[VMEM] * 3,
        out_specs=(VMEM, VMEM),
        compiler_params=limit(1),
        cost_estimate=pl.CostEstimate(flops=0, bytes_accessed=4 << 20, transcendentals=0),
        name="merge_forces",
    )(force, from_above, from_below)
    finished = pl.pallas_call(
        functools.partial(finish_kernel, held),
        out_shape=jax.ShapeDtypeStruct((3, held, points), f32),
        in_specs=[HBM] + [VMEM] * 3,
        out_specs=HBM,
        scratch_shapes=[
            pltpu.VMEM((2, 3, ALIGNED, points), f32),
            pltpu.SemaphoreType.DMA((2,)),
        ],
        input_output_aliases={0: 0},
        compiler_params=limit(1),
        name="finish_ends",
    )(in_hbm(merged.reshape(3, held, points)), blocks, near_force, far_force)
    return jnp.transpose(finished, (1, 0, 2))


def solution(mesh):
    placed = P(("strip", "tile"), None, None)
    return jax.shard_map(
        on_device,
        mesh=mesh,
        in_specs=(placed, placed, P(("strip", "tile"), None), placed),
        out_specs=placed,
        check_vma=False,
    )
```
